256 devices in a mesh: rec: 64 (over x, z, core), rep: 4 (over y).
Axes of the slice: x: 4, y: 4, z: 8, core: 2. Of those that a mesh axis runs over, the one named last changes fastest.
Arguments:
- embeddings: float32 [4, 24576, 1024], P('rep', 'rec'), may hold values from -1 to 1
- weight: bfloat16 [1024, 1024], replicated, may hold values from -1.5 to 1.5
- members: int32 [4, 512, 99], P('rep', 'rec'), may hold values from -1 to 24575, as said below
- pair_slots: int32 [4, 8192, 2], P('rep', 'rec'), may hold values from 0 to 791, as said below
- labels: int32 [4, 8192], P('rep', 'rec'), may hold values 0 or 1
Outputs:
- emb_grad: float32 [4, 24576, 1024], P('rep', 'rec')
- weight_grad: float32 [1024, 1024], P('rec')
The draws below stay inside these ranges and needn't reach their ends.
Inputs may be any that keep to these rules, and one draw needn't show every extreme that they name: `members`: values are records of the same batch. In each block the live slots come first and number 1 to 99; on every index of rec one block has exactly 99. The blocks of one index of rec hold 264 live slots, of which at most 12 name records of one index of rec, and exactly 12 for one of them. A record may stand in several slots. `pair_slots`: both slots of a pair are live and lie in one block of the same index of rec as the pair's row.
All inputs are finite; a program needn't handle non-finite values. No bound on the sum of `labels` on one device may be relied on, other than what follows from the above.
Results may differ from the reference program's by a relative error of at most 0.0065.
Values may be sent and summed in bfloat16 or wider, within the bound.
No kernel may reach another device: no remote copies, remote signals or barrier semaphores. Data moves between devices by JAX's collectives and lax.ppermute only.
A program may use at most 64 MiB of HBM per device.

```python
import jax
import jax.numpy as jnp
from jax import lax

D = 1024
REC_DEV = 384
BLK_DEV = 8
PAIR_DEV = 128
HOT = 8
TOTAL_DEV = 264
MOST = 99
RG = 24576
PAIRS = 8192
GROUPS = 4
N_REC = 64
N_REP = 4


def owner_layout(owner_key):
    subkeys = jax.random.split(owner_key, 7)
    hot_source = jax.random.randint(subkeys[0], (), 0, N_REC)
    member_order = jnp.arange(TOTAL_DEV)
    source_dev = jnp.where(member_order < HOT, hot_source, (member_order - HOT) % N_REC)
    local_row = jax.random.randint(subkeys[1], (TOTAL_DEV,), 0, REC_DEV)
    member_ids = (source_dev * REC_DEV + local_row)[jax.random.permutation(subkeys[2], TOTAL_DEV)]
    rest_count = BLK_DEV - 1
    rest_units = TOTAL_DEV - MOST - rest_count
    base_size = rest_units // rest_count
    extra_units = rest_units % rest_count
    block_sizes = 1 + base_size + (jax.random.permutation(subkeys[3], rest_count) < extra_units).astype(jnp.int32)
    transfers = jax.random.randint(subkeys[4], (rest_count // 2,), 0, base_size + 1)
    for pair_index in range(rest_count // 2):
        block_sizes = block_sizes.at[2 * pair_index].add(transfers[pair_index])
        block_sizes = block_sizes.at[2 * pair_index + 1].add(-transfers[pair_index])
    block_sizes = block_sizes[jax.random.permutation(subkeys[5], rest_count)]
    big_block = jax.random.randint(subkeys[6], (), 0, BLK_DEV)
    block_index = jnp.arange(BLK_DEV)
    shifted = jnp.clip(block_index - (block_index > big_block).astype(jnp.int32), 0, rest_count - 1)
    lengths = jnp.where(block_index == big_block, MOST, block_sizes[shifted]).astype(jnp.int32)
    offsets = jnp.cumsum(lengths) - lengths
    column = jnp.arange(MOST)
    position = jnp.clip(offsets[:, None] + column[None, :], 0, TOTAL_DEV - 1)
    member = jnp.where(column[None, :] < lengths[:, None], member_ids[position], -1).astype(jnp.int32)
    return (lengths, offsets, member)


def owner_keys(key):
    base_key = jax.random.fold_in(key, 7)
    return jax.random.split(base_key, N_REP * N_REC)


def draw_members(key, part):
    subkeys = owner_keys(key)
    lengths, offsets, member = jax.vmap(owner_layout)(subkeys)
    return member.reshape(N_REP, N_REC * BLK_DEV, MOST)


def owner_pairs(owner_key):
    lengths, offsets, member = owner_layout(owner_key)
    pair_key = jax.random.fold_in(owner_key, 11)
    first_key, second_key = jax.random.split(pair_key)
    picked = jax.random.randint(first_key, (PAIR_DEV,), 0, TOTAL_DEV)
    block_of = jnp.sum((offsets[None, :] <= picked[:, None]).astype(jnp.int32), axis=1) - 1
    row_first = picked - offsets[block_of]
    block_len = lengths[block_of]
    step_size = jax.random.randint(second_key, (PAIR_DEV,), 0, jnp.maximum(block_len - 1, 1))
    row_second = (row_first + 1 + step_size) % block_len
    return jnp.stack([block_of * MOST + row_first, block_of * MOST + row_second], axis=1).astype(jnp.int32)


def draw_pair_slots(key, part):
    subkeys = owner_keys(key)
    slots = jax.vmap(owner_pairs)(subkeys)
    return slots.reshape(N_REP, N_REC * PAIR_DEV, 2)


def touch_ends(result, rng, smallest, high):
    spot = [jax.random.randint(jax.random.fold_in(rng, axis), (), 0, length) for axis, length in enumerate(result.shape)]
    main_axis = result.shape.index(max(result.shape))
    beside = spot[:main_axis] + [(spot[main_axis] + 1) % result.shape[main_axis]] + spot[main_axis + 1:]
    return result.at[tuple(spot)].set(smallest).at[tuple(beside)].set(high)


def spiked(drawn, key, source, target, blocks, factor):
    def block_of(dim):
        return (jnp.arange(drawn.shape[dim]) // (drawn.shape[dim] // blocks)).reshape((-1,) + (1,) * (drawn.ndim - 1 - dim))

    one_side = jax.random.permutation(key, blocks)[block_of(target)]
    second = (block_of(target) + blocks // 2) % blocks
    return jnp.where((block_of(source) == one_side) | (block_of(source) == second), factor * drawn, drawn)


def block_levels(rng, shape, cuts, low, largest):
    def one(axis_at, shards_of):
        steps = jax.random.uniform(jax.random.fold_in(jax.random.fold_in(rng, 6), axis_at), (shards_of,), jnp.float32, low / len(cuts), largest / len(cuts))
        return jnp.repeat(jnp.exp(steps), shape[axis_at] // shards_of).reshape((-1,) + (1,) * (len(shape) - axis_at - 1))

    loudness = one(*cuts[0])
    for cut in cuts[1:]:
        loudness = loudness * one(*cut)
    return loudness


def scatter_about(rng, dims, deviation, most, shards=(), dtype=jnp.bfloat16):
    gain = block_levels(rng, dims, shards, -0.22, 0.18) if shards else 1.0
    values = jax.random.normal(rng, dims, jnp.float32) * deviation * gain
    return jnp.minimum(jnp.maximum(values, -most), most).astype(dtype)


def gaussian_with(key, shape, spread, most, shards, heavy, dtype=jnp.bfloat16):
    values = spread * jax.random.normal(key, shape, jnp.float32)
    if shards:
        values = values * block_levels(key, shape, shards, -0.22, 0.18)
    return jnp.clip(spiked(values, jax.random.fold_in(key, 3), *heavy), -most, most).astype(dtype)


def setup_inputs(seed: int = 0) -> dict:
    streams_of = jax.random.split(jax.random.key(seed), 6)
    return {
        "embeddings": gaussian_with(streams_of[0], (GROUPS, RG, D), 0.0625, 1.0, ((0, 4), (1, 64)), (1, 2, 64, 4.0), jnp.float32),
        "weight": scatter_about(streams_of[1], (D, D), 0.25, 1.5),
        "members": draw_members(jax.random.fold_in(streams_of[5], 71), 0),
        "pair_slots": draw_pair_slots(jax.random.fold_in(streams_of[5], 71), 0),
        "labels": touch_ends((jax.random.randint(streams_of[4], (GROUPS, PAIRS), 0, 2) < 1).astype(jnp.int32), jax.random.fold_in(streams_of[4], 1), 0, 1),
    }


margin_shift = 0.5


def owner_terms(rows, live_slot, weight, pair_slots, labels):
    n_blocks, most = live_slot.shape
    feature_dim = rows.shape[1]
    left_proj = jnp.dot(rows, weight, preferred_element_type=jnp.float32).astype(jnp.bfloat16)
    right_proj = lax.dot_general(rows, weight, (((1,), (1,)), ((), ())), preferred_element_type=jnp.float32).astype(jnp.bfloat16)
    rows_three = rows.reshape(n_blocks, most, feature_dim).astype(jnp.float32)
    left_three = left_proj.reshape(n_blocks, most, feature_dim).astype(jnp.float32)
    right_three = right_proj.reshape(n_blocks, most, feature_dim).astype(jnp.float32)
    scores = jnp.einsum("bmd,bnd->bmn", left_three, rows_three)
    counts = jnp.sum(live_slot.astype(jnp.float32), axis=1)
    positions = jnp.arange(most)
    pair_live = live_slot[:, :, None] & live_slot[:, None, :] & (positions[:, None] != positions[None, :])
    grad_full = jnp.where(pair_live, jax.nn.sigmoid(scores - margin_shift) / counts[:, None, None], jnp.zeros_like(scores))
    first_slot = pair_slots[:, 0]
    second_slot = pair_slots[:, 1]
    block_of = (first_slot // most).astype(jnp.int32)
    row_first = (first_slot % most).astype(jnp.int32)
    row_second = (second_slot % most).astype(jnp.int32)
    signs = (1 - 2 * labels).astype(jnp.float32)
    picked = scores[block_of, row_first, row_second]
    grad_full = grad_full.at[block_of, row_first, row_second].add(signs * jax.nn.sigmoid(signs * (picked - margin_shift)))
    grad_bf = grad_full.astype(jnp.bfloat16).astype(jnp.float32)
    slot_grad = jnp.einsum("bmn,bnd->bmd", grad_bf, right_three) + jnp.einsum("bnm,bnd->bmd", grad_bf, left_three)
    slot_grad = slot_grad.astype(jnp.bfloat16)
    carried = jnp.einsum("bmn,bnd->bmd", grad_bf, rows_three).astype(jnp.bfloat16)
    weight_term = lax.dot_general(rows, carried.reshape(-1, feature_dim), (((0,), (0,)), ((), ())), preferred_element_type=jnp.float32)
    return slot_grad.reshape(-1, feature_dim), weight_term


def reference(embeddings, weight, members, pair_slots, labels):
    feature_dim = embeddings.shape[2]
    grads_all = []
    weight_sum = jnp.zeros((feature_dim, feature_dim), jnp.float32)
    for group in range(N_REP):
        row_table = embeddings[group].astype(jnp.bfloat16)
        record_count = row_table.shape[0]
        member_table = members[group].reshape(N_REC, BLK_DEV, -1)
        pair_table = pair_slots[group].reshape(N_REC, PAIR_DEV, 2)
        label_table = labels[group].reshape(N_REC, PAIR_DEV)

        def owner_step(summed, inputs):
            member_ids, pairs_now, labels_now = inputs
            live_slot = member_ids >= 0
            flat_ids = member_ids.reshape(-1)
            gathered = row_table[jnp.maximum(flat_ids, 0).astype(jnp.int32)]
            rows = jnp.where(live_slot.reshape(-1)[:, None], gathered, jnp.zeros_like(gathered))
            slot_grad, weight_term = owner_terms(rows, live_slot, weight, pairs_now, labels_now)
            return summed + weight_term, slot_grad

        weight_sum, slot_grads = lax.scan(owner_step, weight_sum, (member_table, pair_table, label_table))
        flat_members = members[group].reshape(-1)
        target = jnp.where(flat_members >= 0, flat_members, record_count).astype(jnp.int32)
        grad_rows = jnp.zeros((record_count, feature_dim), jnp.float32).at[target].add(slot_grads.reshape(-1, feature_dim).astype(jnp.float32), mode="drop")
        grads_all.append(grad_rows)
    return jnp.stack(grads_all), weight_sum
```

```python
import jax
import jax.numpy as jnp
from jax import lax
from jax.experimental import pallas as pl
from jax.experimental.pallas import tpu as pltpu
from jax.sharding import Mesh, PartitionSpec as P

f32, bf16, i32 = jnp.float32, jnp.bfloat16, jnp.int32

CAP = 12
LIVE = 264
SUB = 272
LAN = 384
MARGIN = 0.5
NX, NZ, NC, NY = 4, 8, 2, 4
REC = ("x", "z", "c")
MIB = 2**20


def iota(shape, dim):
    return lax.broadcasted_iota(i32, shape, dim)


def ones_where(mask):
    return jnp.where(mask, 1.0, 0.0).astype(f32)


def nt(a, b):
    return lax.dot_general(a, b, (((1,), (1,)), ((), ())), preferred_element_type=f32)


def tn(a, b):
    return lax.dot_general(a, b, (((0,), (0,)), ((), ())), preferred_element_type=f32)


def mm(a, b):
    return jnp.dot(a, b, preferred_element_type=f32)


def bucket_tables(members_ref, padded, n_rec, rec_rows):
    blocks, most = members_ref.shape
    padded[...] = jnp.full(padded.shape, -1, i32)
    padded[:, :most] = members_ref[...]
    earlier = ones_where(iota((128, 128), 0) < iota((128, 128), 1)).astype(bf16)
    running = jnp.zeros((n_rec, 1), f32)
    out = []
    for b in range(blocks):
        ids = padded[b : b + 1, :]
        source = (lax.shift_right_arithmetic(ids, 7) * 171) >> 9
        row = ids - source * rec_rows
        source = jnp.where(ids >= 0, source, -1)
        hit = ones_where(iota((n_rec, 128), 0) == source)
        place = mm(hit.astype(bf16), earlier) + running
        running = running + jnp.sum(hit, axis=1, keepdims=True)
        out.append((source, row, hit, place))
    return out


def request_kernel(members_ref, out_ref, padded):
    n_rec = out_ref.shape[0]
    tables = bucket_tables(members_ref, padded, n_rec, LAN)
    lane = iota((n_rec, 128), 1)
    asked = jnp.zeros((n_rec, 128), f32)
    for k in range(CAP):
        found = jnp.zeros((n_rec, 128), f32)
        for source, row, hit, place in tables:
            found = found + jnp.where(place == k, hit, 0.0) * (row + 1).astype(f32)
        asked = jnp.where(lane == k, jnp.sum(found, axis=1, keepdims=True), asked)
    out_ref[...] = asked.astype(i32).reshape(out_ref.shape)


def fetch_kernel(asked_ref, emb_ref, out_ref, pick_ref):
    n_rec = asked_ref.shape[0]
    half = out_ref.shape[1]
    rows = n_rec * 2 * CAP
    asked = asked_ref[...].reshape(n_rec, 1, 128).astype(f32)
    step = iota((n_rec, 2 * CAP, 128), 1)
    step = jnp.where(step >= CAP, step - CAP, step)
    mine = jnp.where(iota((n_rec, 2 * CAP, 128), 2) == step, asked, 0.0)
    wanted = jnp.sum(mine, axis=2, keepdims=True).astype(i32) - 1
    wanted = wanted + jnp.where(iota((n_rec, 2 * CAP, 1), 1) >= CAP, jnp.where(wanted >= 0, LAN, 0), 0)
    pick = ones_where(iota((n_rec, 2 * CAP, 2 * LAN), 2) == wanted).reshape(rows, 2 * LAN).astype(bf16)
    pick_ref[...] = pick
    left = emb_ref[:, :half].astype(bf16)
    right = emb_ref[:, half:].astype(bf16)
    out_ref[...] = mm(pick, jnp.concatenate([left, right], axis=0)).astype(bf16)


def prepare_kernel(members_ref, pairs_ref, labels_ref, gather_ref, spread_ref, share_ref, plus_ref, minus_ref, padded):
    n_rec = gather_ref.shape[1] // (2 * CAP)
    blocks, most = members_ref.shape
    tables = bucket_tables(members_ref, padded, n_rec, LAN)
    sub = iota((LAN, 128), 0)
    lane = iota((1, 128), 1)
    offset = jnp.zeros((1, 1), i32)
    offsets, lengths = [], []
    bucket = jnp.zeros((LAN, 1), f32)
    for b, (source, row, hit, place) in enumerate(tables):
        live = source >= 0
        length = jnp.sum(ones_where(live), axis=1, keepdims=True).astype(i32)
        offsets.append(offset)
        lengths.append(length)
        slot = jnp.where(live, offset + lane, -1)
        offset = offset + length
        at = jnp.sum(hit * place, axis=0, keepdims=True) + (source * (2 * CAP) + 1).astype(f32)
        bucket = bucket + jnp.sum(jnp.where(sub == slot, at, 0.0), axis=1, keepdims=True)
    bucket_col = bucket.astype(i32) - 1
    bucket_col = jnp.where(bucket_col < 0, -4096, bucket_col)
    bucket_row = jnp.transpose(jnp.broadcast_to(bucket, (LAN, 128)))[0:1, :].astype(i32) - 1
    bucket_row = jnp.where(bucket_row < 0, -4096, bucket_row)
    arrivals = gather_ref.shape[1]
    lanes = iota((SUB, arrivals), 1)
    gather_ref[:SUB, :] = ones_where(lanes == bucket_col[:SUB]).astype(bf16)
    gather_ref[SUB:, :] = ones_where(lanes == bucket_col[:SUB] + CAP).astype(bf16)
    rows = iota((arrivals, LAN), 0)
    spread_ref[:, :LAN] = ones_where(rows == bucket_row).astype(bf16)
    spread_ref[:, LAN:] = ones_where(rows == bucket_row + CAP).astype(bf16)

    col, row = iota((SUB, 1), 0), iota((1, LAN), 1)
    block_col, block_row = jnp.zeros((SUB, 1), i32), jnp.zeros((1, LAN), i32)
    count = jnp.zeros((1, LAN), f32) + lengths[0].astype(f32)
    for b in range(1, blocks):
        block_col = jnp.where(col >= offsets[b], b, block_col)
        block_row = jnp.where(row >= offsets[b], b, block_row)
        count = jnp.where(row >= offsets[b], lengths[b].astype(f32), count)
    block_col = jnp.where(col < LIVE, block_col, -1)
    block_row = jnp.where(row < LIVE, block_row, -2)
    inverse = 1.0 / count
    share_ref[...] = jnp.where((block_col == block_row) & (col != row), inverse, 0.0)

    def packed(slots):
        at = jnp.zeros((1, 128), i32) + offsets[0]
        first = jnp.zeros((1, 128), i32)
        for b in range(1, blocks):
            at = jnp.where(slots >= b * most, offsets[b], at)
            first = jnp.where(slots >= b * most, b * most, first)
        return at + slots - first

    label = labels_ref[...].astype(f32)
    one = jnp.where(iota((SUB, 128), 0) == packed(pairs_ref[0:1, :]), 1.0, 0.0)
    two = ones_where(iota((LAN, 128), 0) == packed(pairs_ref[1:2, :])).astype(bf16)
    plus_ref[...] = nt((one * (1.0 - label)).astype(bf16), two)
    minus_ref[...] = nt((one * label).astype(bf16), two)


def owner_kernel(
    arrived_ref, gather_ref, spread_ref, share_ref, plus_ref, minus_ref, weight_ref,
    out_ref, rows_ref, dscore_ref, right_s, stacked_s,
):
    half = arrived_ref.shape[1]
    both = mm(gather_ref[...], arrived_ref[...]).astype(bf16)
    rows_ref[:SUB, :half] = both[:SUB]
    rows_ref[:SUB, half:] = both[SUB:]
    rows_ref[SUB:, :] = jnp.zeros((LAN - SUB, 2 * half), bf16)
    rows = rows_ref[:SUB, :]
    left = mm(rows, weight_ref[...]).astype(bf16)
    right_s[:SUB, :] = nt(rows, weight_ref[...]).astype(bf16)
    right_s[SUB:, :] = jnp.zeros((LAN - SUB, 2 * half), bf16)
    shifted = nt(left, rows_ref[...]) - MARGIN
    small = jnp.exp(-jnp.abs(shifted))
    larger = 1.0 / (1.0 + small)
    smaller = small * larger
    up = jnp.where(shifted >= 0, larger, smaller)
    down = jnp.where(shifted >= 0, smaller, larger)
    dscore = (up * share_ref[...] + (up * plus_ref[...] - down * minus_ref[...])).astype(bf16)
    dscore_ref[...] = dscore
    grad = mm(dscore, right_s[...]) + tn(dscore, left)[:SUB]
    grad = grad.astype(bf16)
    stacked_s[:SUB, :] = grad[:, :half]
    stacked_s[SUB:LAN, :] = jnp.zeros((LAN - SUB, half), bf16)
    stacked_s[LAN : LAN + SUB, :] = grad[:, half:]
    stacked_s[LAN + SUB :, :] = jnp.zeros((LAN - SUB, half), bf16)
    out_ref[...] = mm(spread_ref[...], stacked_s[...]).astype(bf16)


def weight_kernel(core_ref, rows_ref, dscore_ref, keep_ref, send_ref):
    width = rows_ref.shape[1]
    core = core_ref[0]
    carried = mm(dscore_ref[...], rows_ref[...]).astype(bf16)
    tile = 256
    for t in range(width // tile):
        part = tn(rows_ref[:SUB, t * tile : (t + 1) * tile], carried)
        part = part.reshape(tile // 32, 2, 16, width)
        even = jnp.broadcast_to(core, (tile // 32, 16, width)) == 0
        keep_ref[t * 8 : (t + 1) * 8] = jnp.where(even, part[:, 0], part[:, 1])
        send_ref[t * 8 : (t + 1) * 8] = jnp.where(even, part[:, 1], part[:, 0]).astype(bf16)


def return_kernel(pick_ref, back_ref, out_ref):
    half = back_ref.shape[1]
    total = mm(pick_ref[...], back_ref[...])
    rec_rows = out_ref.shape[0]
    out_ref[:, :half] = total[:rec_rows]
    out_ref[:, half:] = total[rec_rows:]


def vmem(n):
    return [pl.BlockSpec(memory_space=pltpu.VMEM)] * n


def call(kernel, outs, n_in, scratch=(), flops=0, moved=0, smem=0):
    single = not isinstance(outs, (list, tuple))
    return pl.pallas_call(
        kernel,
        out_shape=outs,
        in_specs=[pl.BlockSpec(memory_space=pltpu.SMEM)] * smem + vmem(n_in),
        out_specs=vmem(1)[0] if single else vmem(len(outs)),
        scratch_shapes=list(scratch),
        compiler_params=pltpu.CompilerParams(vmem_limit_bytes=40 * MIB),
        cost_estimate=pl.CostEstimate(flops=flops, bytes_accessed=moved, transcendentals=0),
    )


def shifted_blocks(value, axis, size):
    here = lax.axis_index(axis)
    got = []
    for k in range(1, size):
        block = lax.dynamic_index_in_dim(value, (here + k) % size, 0, keepdims=False).astype(bf16)
        got.append(lax.ppermute(block, axis, [(i, (i + k) % size) for i in range(size)]))
    total = lax.dynamic_index_in_dim(value, here, 0, keepdims=False)
    for block in got:
        total = total + block.astype(f32)
    return total


def on_device(embeddings, weight, members, pair_slots, labels):
    n_rec = NX * NZ * NC
    rec_rows, width = embeddings.shape[1:]
    half = width // 2
    arrivals = n_rec * 2 * CAP
    struct = jax.ShapeDtypeStruct
    ids = members[0]
    padded = pltpu.VMEM((ids.shape[0], 128), i32)

    requests = call(request_kernel, struct((n_rec, 1, 128), i32), 1, [padded])(ids)
    asked = lax.all_to_all(requests, REC, split_axis=0, concat_axis=0, tiled=True)
    found, pick = call(
        fetch_kernel, [struct((arrivals, half), bf16), struct((arrivals, 2 * rec_rows), bf16)], 2,
        flops=4 * arrivals * rec_rows * half, moved=6 * MIB,
    )(asked, embeddings[0])
    arrived = lax.all_to_all(
        found.reshape(n_rec, 2 * CAP, half), REC, split_axis=0, concat_axis=0, tiled=True
    ).reshape(arrivals, half)
    gather, spread, share, plus, minus = call(
        prepare_kernel,
        [struct((2 * SUB, arrivals), bf16), struct((arrivals, 2 * LAN), bf16)] + [struct((SUB, LAN), f32)] * 3,
        3, [padded], moved=6 * MIB,
    )(ids, pair_slots[0].T, labels)
    pick_t = pick.T

    out, rows, dscore = call(
        owner_kernel,
        [struct((arrivals, half), bf16), struct((LAN, width), bf16), struct((SUB, LAN), bf16)],
        7,
        [pltpu.VMEM((LAN, width), bf16), pltpu.VMEM((2 * LAN, half), bf16)],
        flops=4 * 10**9, moved=12 * MIB,
    )(arrived, gather, spread, share, plus, minus, weight)
    returned = lax.all_to_all(
        out.reshape(n_rec, 2 * CAP, half), REC, split_axis=0, concat_axis=0, tiled=True
    ).reshape(arrivals, half)

    core = lax.axis_index("c").astype(i32).reshape(1)
    shares = NX * NZ
    keep, send = call(
        weight_kernel, [struct((shares, 16, width), f32), struct((shares, 16, width), bf16)], 2,
        flops=10**9, moved=8 * MIB, smem=1,
    )(core, rows, dscore)
    got = lax.ppermute(send, "c", [(0, 1), (1, 0)])
    summed = (keep + got.astype(f32)).reshape(shares * 16, NY, width // NY).swapaxes(0, 1)
    summed = shifted_blocks(summed, "y", NY)
    summed = shifted_blocks(summed.reshape(NX, NZ * 16, width // NY), "x", NX)
    summed = shifted_blocks(summed.reshape(NZ, 16, width // NY), "z", NZ)
    weight_part = lax.all_gather(summed, "y", axis=1, tiled=True)

    emb_grad = call(
        return_kernel, struct((rec_rows, width), f32), 2,
        flops=4 * arrivals * rec_rows * half, moved=6 * MIB,
    )(pick_t, returned)
    return (emb_grad[None], weight_part)


def solution(mesh):
    fine = Mesh(mesh.devices.reshape(NX, NZ, NC, NY), ("x", "z", "c", "y"))
    return jax.shard_map(
        on_device,
        mesh=fine,
        in_specs=(
            P("y", REC, None),
            P(),
            P("y", REC, None),
            P("y", REC, None),
            P("y", REC),
        ),
        out_specs=(P("y", REC, None), P(REC, None)),
        check_vma=False,
    )
```

```python
import jax
import jax.numpy as jnp
from jax import lax
from jax.experimental import pallas as pl
from jax.experimental.pallas import tpu as pltpu
from jax.sharding import Mesh, PartitionSpec as P

f32, bf16, i32 = jnp.float32, jnp.bfloat16, jnp.int32

CAP = 12
LIVE = 264
SUB = 272
LAN = 384
MARGIN = 0.5
NX, NZ, NC, NY = 4, 8, 2, 4
REC = ("x", "z", "c")
MIB = 2**20


def iota(shape, dim):
    return lax.broadcasted_iota(i32, shape, dim)


def ones_where(mask):
    return jnp.where(mask, 1.0, 0.0).astype(f32)


def nt(a, b):
    return lax.dot_general(a, b, (((1,), (1,)), ((), ())), preferred_element_type=f32)


def tn(a, b):
    return lax.dot_general(a, b, (((0,), (0,)), ((), ())), preferred_element_type=f32)


def mm(a, b):
    return jnp.dot(a, b, preferred_element_type=f32)


def bucket_tables(members_ref, padded, n_rec, rec_rows):
    blocks, most = members_ref.shape
    padded[...] = jnp.full(padded.shape, -1, i32)
    padded[:, :most] = members_ref[...]
    earlier = ones_where(iota((128, 128), 0) < iota((128, 128), 1)).astype(bf16)
    running = jnp.zeros((n_rec, 1), f32)
    out = []
    for b in range(blocks):
        ids = padded[b : b + 1, :]
        source = (lax.shift_right_arithmetic(ids, 7) * 171) >> 9
        row = ids - source * rec_rows
        source = jnp.where(ids >= 0, source, -1)
        hit = ones_where(iota((n_rec, 128), 0) == source)
        place = mm(hit.astype(bf16), earlier) + running
        running = running + jnp.sum(hit, axis=1, keepdims=True)
        out.append((source, row, hit, place))
    return out


def request_kernel(members_ref, out_ref, padded):
    n_rec = out_ref.shape[0]
    tables = bucket_tables(members_ref, padded, n_rec, LAN)
    lane = iota((n_rec, 128), 1)
    asked = jnp.zeros((n_rec, 128), f32)
    for k in range(CAP):
        found = jnp.zeros((n_rec, 128), f32)
        for source, row, hit, place in tables:
            found = found + jnp.where(place == k, hit, 0.0) * (row + 1).astype(f32)
        asked = jnp.where(lane == k, jnp.sum(found, axis=1, keepdims=True), asked)
    out_ref[...] = asked.astype(i32).reshape(out_ref.shape)


def wanted_rows(asked_ref):
    n_rec = asked_ref.shape[0]
    asked = asked_ref[...].reshape(n_rec, 1, 128).astype(f32)
    step = iota((n_rec, 2 * CAP, 128), 1)
    step = jnp.where(step >= CAP, step - CAP, step)
    mine = jnp.where(iota((n_rec, 2 * CAP, 128), 2) == step, asked, 0.0)
    wanted = jnp.sum(mine, axis=2, keepdims=True).astype(i32) - 1
    later = iota((n_rec, 2 * CAP, 1), 1) >= CAP
    return wanted + jnp.where(later & (wanted >= 0), LAN, 0)


def fetch_kernel(asked_ref, emb_ref, out_ref, table, sem):
    n_rec = asked_ref.shape[0]
    half = out_ref.shape[1]
    rows = n_rec * 2 * CAP
    load = pltpu.make_async_copy(emb_ref, table, sem)
    load.start()
    wanted = wanted_rows(asked_ref)
    pick = ones_where(iota((n_rec, 2 * CAP, 2 * LAN), 2) == wanted).reshape(rows, 2 * LAN).astype(bf16)
    load.wait()
    left = table[:, :half].astype(bf16)
    right = table[:, half:].astype(bf16)
    out_ref[...] = mm(pick, jnp.concatenate([left, right], axis=0)).astype(bf16)


def prepare_kernel(
    members_ref, pairs_ref, labels_ref, asked_ref,
    gather_ref, table_ref, back_ref, padded,
):
    arrivals = gather_ref.shape[1]
    n_rec = arrivals // (2 * CAP)
    blocks, most = members_ref.shape
    tables = bucket_tables(members_ref, padded, n_rec, LAN)
    sub = iota((LAN, 128), 0)
    lane = iota((1, 128), 1)
    offset = jnp.zeros((1, 1), i32)
    offsets, lengths = [], []
    bucket = jnp.zeros((LAN, 1), f32)
    for b, (source, row, hit, place) in enumerate(tables):
        live = source >= 0
        length = jnp.sum(ones_where(live), axis=1, keepdims=True).astype(i32)
        offsets.append(offset)
        lengths.append(length)
        slot = jnp.where(live, offset + lane, -1)
        offset = offset + length
        at = jnp.sum(hit * place, axis=0, keepdims=True) + (source * (2 * CAP) + 1).astype(f32)
        bucket = bucket + jnp.sum(jnp.where(sub == slot, at, 0.0), axis=1, keepdims=True)
    bucket_col = bucket.astype(i32) - 1
    bucket_col = jnp.where(bucket_col < 0, -4096, bucket_col)
    bucket_row = jnp.transpose(jnp.broadcast_to(bucket, (LAN, 128)))[0:1, :].astype(i32) - 1
    bucket_row = jnp.where(bucket_row < 0, -4096, bucket_row)
    lanes = iota((SUB, arrivals), 1)
    gather_ref[:SUB, :] = ones_where(lanes == bucket_col[:SUB]).astype(bf16)
    gather_ref[SUB:, :] = ones_where(lanes == bucket_col[:SUB] + CAP).astype(bf16)
    rows = iota((arrivals, LAN), 0)
    table_ref[:arrivals, :LAN] = ones_where(rows == bucket_row).astype(bf16)
    table_ref[:arrivals, LAN:] = ones_where(rows == bucket_row + CAP).astype(bf16)

    col, row = iota((SUB, 1), 0), iota((1, LAN), 1)
    block_col, block_row = jnp.zeros((SUB, 1), i32), jnp.zeros((1, LAN), i32)
    count = jnp.zeros((1, LAN), f32) + lengths[0].astype(f32)
    for b in range(1, blocks):
        block_col = jnp.where(col >= offsets[b], b, block_col)
        block_row = jnp.where(row >= offsets[b], b, block_row)
        count = jnp.where(row >= offsets[b], lengths[b].astype(f32), count)
    block_col = jnp.where(col < LIVE, block_col, -1)
    block_row = jnp.where(row < LIVE, block_row, -2)
    counts = jnp.where((block_col == block_row) & (col != row), count, 0.0)
    table_ref[arrivals : arrivals + SUB, :LAN] = counts.astype(bf16)

    def packed(slots):
        at = jnp.zeros((1, 128), i32) + offsets[0]
        first = jnp.zeros((1, 128), i32)
        for b in range(1, blocks):
            at = jnp.where(slots >= b * most, offsets[b], at)
            first = jnp.where(slots >= b * most, b * most, first)
        return at + slots - first

    label = labels_ref[...].astype(f32)
    one = jnp.where(iota((SUB, 128), 0) == packed(pairs_ref[0:1, :]), 1.0, 0.0)
    two = ones_where(iota((LAN, 128), 0) == packed(pairs_ref[1:2, :])).astype(bf16)
    table_ref[arrivals : arrivals + SUB, LAN:] = nt((one * (1.0 - label)).astype(bf16), two).astype(bf16)
    table_ref[arrivals + SUB :, :LAN] = nt((one * label).astype(bf16), two).astype(bf16)
    table_ref[arrivals + SUB :, LAN:] = jnp.zeros((SUB, LAN), bf16)
    wanted = wanted_rows(asked_ref).reshape(arrivals, 1).astype(f32)
    wanted = jnp.transpose(jnp.broadcast_to(wanted, (arrivals, 128)))[0:1, :].astype(i32)
    back_ref[...] = ones_where(iota((2 * LAN, arrivals), 0) == wanted).astype(bf16)


def owner_kernel(
    core_ref, arrived_ref, gather_hbm, weight_hbm, table_hbm,
    out_ref, keep_ref, send_ref,
    gather_s, rows_s, right_s, stacked_s, weight_s, spread_s, terms_s, sems,
):
    arrivals, half = arrived_ref.shape
    width = 2 * half
    terms_hbm, spread_hbm = table_hbm.at[arrivals:], table_hbm.at[:arrivals]
    loads = []
    for n, (source, target) in enumerate(
        [(gather_hbm, gather_s), (weight_hbm, weight_s), (terms_hbm, terms_s), (spread_hbm, spread_s)]
    ):
        loads.append(pltpu.make_async_copy(source, target, sems.at[n]))
        loads[n].start()
    loads[0].wait()
    both = mm(gather_s[...], arrived_ref[...]).astype(bf16)
    rows_s[:SUB, :half] = both[:SUB]
    rows_s[:SUB, half:] = both[SUB:]
    rows_s[SUB:, :] = jnp.zeros((LAN - SUB, width), bf16)
    rows = rows_s[:SUB, :]
    loads[1].wait()
    left = mm(rows, weight_s[...]).astype(bf16)
    right_s[:SUB, :] = nt(rows, weight_s[...]).astype(bf16)
    right_s[SUB:, :] = jnp.zeros((LAN - SUB, width), bf16)
    shifted = nt(left, rows_s[...]) - MARGIN
    small = jnp.exp(-jnp.abs(shifted))
    larger = 1.0 / (1.0 + small)
    smaller = small * larger
    up = jnp.where(shifted >= 0, larger, smaller)
    down = jnp.where(shifted >= 0, smaller, larger)
    loads[2].wait()
    count = terms_s[:SUB, :LAN].astype(f32)
    plus = terms_s[:SUB, LAN:].astype(f32)
    minus = terms_s[SUB:, :LAN].astype(f32)
    dscore = jnp.where(count > 0, up / jnp.maximum(count, 1.0), 0.0) + (up * plus - down * minus)
    dscore = dscore.astype(bf16)
    grad = mm(dscore, right_s[...]) + tn(dscore, left)[:SUB]
    grad = grad.astype(bf16)
    stacked_s[:SUB, :] = grad[:, :half]
    stacked_s[SUB:LAN, :] = jnp.zeros((LAN - SUB, half), bf16)
    stacked_s[LAN : LAN + SUB, :] = grad[:, half:]
    stacked_s[LAN + SUB :, :] = jnp.zeros((LAN - SUB, half), bf16)
    loads[3].wait()
    out_ref[...] = mm(spread_s[...], stacked_s[...]).astype(bf16)
    carried = mm(dscore, rows_s[...]).astype(bf16)
    core = core_ref[0]
    tile = 256
    for t in range(width // tile):
        part = tn(rows_s[:SUB, t * tile : (t + 1) * tile], carried)
        part = part.reshape(tile // 32, 2, 16, width)
        even = jnp.broadcast_to(core, (tile // 32, 16, width)) == 0
        here = jnp.where(even, part[:, 0], part[:, 1]).reshape(tile // 2, width)
        there = jnp.where(even, part[:, 1], part[:, 0]).reshape(tile // 2, width)
        keep_ref[t * tile // 2 : (t + 1) * tile // 2, :] = here
        send_ref[t * tile // 2 : (t + 1) * tile // 2, :] = there.astype(bf16)


def split_kernel(y_ref, keep_ref, got_ref, own_ref, *send_refs):
    size = own_ref.shape[1]
    for k in range(NY):
        at = pl.multiple_of(((y_ref[0] + k) % NY) * size, size)
        part = keep_ref[:, pl.ds(at, size)] + got_ref[:, pl.ds(at, size)].astype(f32)
        if k == 0:
            own_ref[...] = part
        else:
            send_refs[k - 1][...] = part.astype(bf16)


def join_kernel(y_ref, *refs):
    *piece_refs, out_ref = refs
    size = piece_refs[0].shape[1]
    for k, piece_ref in enumerate(piece_refs):
        at = pl.multiple_of(((y_ref[0] + NY - k) % NY) * size, size)
        out_ref[:, pl.ds(at, size)] = piece_ref[...]


def return_kernel(back_ref, pick_hbm, out_ref, pick_s, sem):
    half = back_ref.shape[1]
    load = pltpu.make_async_copy(pick_hbm, pick_s, sem)
    load.start()
    load.wait()
    total = mm(pick_s[...], back_ref[...])
    rec_rows = out_ref.shape[0]
    out_ref[:, :half] = total[:rec_rows]
    out_ref[:, half:] = total[rec_rows:]


def vmem(n):
    return [pl.BlockSpec(memory_space=pltpu.VMEM)] * n


def call(kernel, outs, n_in, scratch=(), flops=0, moved=0, smem=0, hbm=0, grant=60):
    single = not isinstance(outs, (list, tuple))
    return pl.pallas_call(
        kernel,
        out_shape=outs,
        in_specs=[pl.BlockSpec(memory_space=pltpu.SMEM)] * smem + vmem(n_in) + [pl.BlockSpec(memory_space=pltpu.HBM)] * hbm,
        out_specs=vmem(1)[0] if single else vmem(len(outs)),
        scratch_shapes=list(scratch),
        compiler_params=pltpu.CompilerParams(vmem_limit_bytes=int(grant * MIB)),
        cost_estimate=pl.CostEstimate(flops=flops, bytes_accessed=moved, transcendentals=0),
    )


def shifted_blocks(value, axis, size):
    here = lax.axis_index(axis)
    got = []
    for k in range(1, size):
        block = lax.dynamic_index_in_dim(value, (here + k) % size, 0, keepdims=False).astype(bf16)
        got.append(lax.ppermute(block, axis, [(i, (i + k) % size) for i in range(size)]))
    total = lax.dynamic_index_in_dim(value, here, 0, keepdims=False)
    for block in got:
        total = total + block.astype(f32)
    return total


def on_device(embeddings, weight, members, pair_slots, labels):
    n_rec = NX * NZ * NC
    rec_rows, width = embeddings.shape[1:]
    half = width // 2
    arrivals = n_rec * 2 * CAP
    struct = jax.ShapeDtypeStruct
    ids = members[0]
    padded = pltpu.VMEM((ids.shape[0], 128), i32)

    requests = call(request_kernel, struct((n_rec, 1, 128), i32), 1, [padded])(ids)
    asked = lax.all_to_all(requests, REC, split_axis=0, concat_axis=0, tiled=True)
    dma = pltpu.SemaphoreType.DMA
    found = call(
        fetch_kernel, struct((arrivals, half), bf16), 1,
        [pltpu.VMEM((rec_rows, width), f32), dma],
        flops=4 * arrivals * rec_rows * half, moved=4 * MIB, hbm=1,
    )(asked, embeddings[0])
    arrived = lax.all_to_all(
        found.reshape(n_rec, 2 * CAP, half), REC, split_axis=0, concat_axis=0, tiled=True
    ).reshape(arrivals, half)
    gather, table, back = call(
        prepare_kernel,
        [
            struct((2 * SUB, arrivals), bf16),
            struct((arrivals + 2 * SUB, 2 * LAN), bf16),
            struct((2 * LAN, arrivals), bf16),
        ],
        4, [padded], moved=8 * MIB,
    )(ids, pair_slots[0].T, labels, asked)

    core = lax.axis_index("c").astype(i32).reshape(1)
    rows_core = width // NC
    out, keep, send = call(
        owner_kernel,
        [struct((arrivals, half), bf16), struct((rows_core, width), f32), struct((rows_core, width), bf16)],
        1,
        [pltpu.VMEM((2 * SUB, arrivals), bf16)]
        + [pltpu.VMEM((LAN, width), bf16)] * 2
        + [pltpu.VMEM((2 * LAN, half), bf16), pltpu.VMEM((width, width), bf16), pltpu.VMEM((arrivals, 2 * LAN), bf16)]
        + [pltpu.VMEM((2 * SUB, 2 * LAN), bf16)]
        + [dma((4,))],
        flops=5 * 10**9, moved=12 * MIB, smem=1, hbm=3, grant=49.5,
    )(core, arrived, gather, weight, table)
    got = lax.ppermute(send, "c", [(0, 1), (1, 0)])
    returned = lax.all_to_all(
        out.reshape(n_rec, 2 * CAP, half), REC, split_axis=0, concat_axis=0, tiled=True
    ).reshape(arrivals, half)

    y = lax.axis_index("y").astype(i32).reshape(1)
    cols = width // NY
    summed, *sends = call(
        split_kernel,
        [struct((rows_core, cols), f32)] + [struct((rows_core, cols), bf16)] * (NY - 1), 2,
        flops=10**6, moved=4 * MIB, smem=1, grant=16,
    )(y, keep, got)
    for k in range(1, NY):
        summed = summed + lax.ppermute(sends[k - 1], "y", [(i, (i + k) % NY) for i in range(NY)]).astype(f32)
    summed = shifted_blocks(summed.reshape(NX, NZ * 16, cols), "x", NX)
    half_z = NZ // 2
    z = lax.axis_index("z")
    summed = summed.reshape(2, half_z, 16, cols)
    far = lax.dynamic_index_in_dim(summed, 1 - z // half_z, 0, keepdims=False).astype(bf16)
    near = lax.dynamic_index_in_dim(summed, z // half_z, 0, keepdims=False)
    far = lax.ppermute(far, "z", [(i, (i + half_z) % NZ) for i in range(NZ)])
    summed = near + far.astype(f32)
    blocks = []
    for k in range(1, half_z):
        block = lax.dynamic_index_in_dim(summed, (z + k) % half_z, 0, keepdims=False).astype(bf16)
        to = [(i, i // half_z * half_z + (i + k) % half_z) for i in range(NZ)]
        blocks.append(lax.ppermute(block, "z", to))
    summed = lax.dynamic_index_in_dim(summed, z % half_z, 0, keepdims=False)
    for block in blocks:
        summed = summed + block.astype(f32)
    pieces = [summed]
    for k in range(1, NY):
        pieces.append(lax.ppermute(summed, "y", [(i, (i + k) % NY) for i in range(NY)]))
    emb_grad = call(
        return_kernel, struct((rec_rows, width), f32), 1, [pltpu.VMEM((2 * rec_rows, arrivals), bf16), dma],
        flops=4 * arrivals * rec_rows * half, moved=6 * MIB, hbm=1, grant=52,
    )(returned, back)
    emb_grad, pieces = lax.optimization_barrier((emb_grad, pieces))
    weight_part = call(join_kernel, struct((16, width), f32), NY, smem=1, flops=10**4, moved=10**5, grant=16)(y, *pieces)

    return (emb_grad[None], weight_part)


def solution(mesh):
    fine = Mesh(mesh.devices.reshape(NX, NZ, NC, NY), ("x", "z", "c", "y"))
    return jax.shard_map(
        on_device,
        mesh=fine,
        in_specs=(
            P("y", REC, None),
            P(),
            P("y", REC, None),
            P("y", REC, None),
            P("y", REC),
        ),
        out_specs=(P("y", REC, None), P(REC, None)),
        check_vma=False,
    )
```

```python
import jax
import jax.numpy as jnp
from jax import lax
from jax.experimental import pallas as pl
from jax.experimental.pallas import tpu as pltpu
from jax.sharding import Mesh, PartitionSpec as P

f32, bf16, i32 = jnp.float32, jnp.bfloat16, jnp.int32

CAP = 12
LIVE = 264
SUB = 272
LAN = 384
MARGIN = 0.5
NX, NZ, NC, NY = 4, 8, 2, 4
REC = ("x", "z", "c")
MIB = 2**20


def iota(shape, dim):
    return lax.broadcasted_iota(i32, shape, dim)


def ones_where(mask):
    return jnp.where(mask, 1.0, 0.0).astype(f32)


def nt(a, b):
    return lax.dot_general(a, b, (((1,), (1,)), ((), ())), preferred_element_type=f32)


def tn(a, b):
    return lax.dot_general(a, b, (((0,), (0,)), ((), ())), preferred_element_type=f32)


def mm(a, b):
    return jnp.dot(a, b, preferred_element_type=f32)


def bucket_tables(members_ref, padded, n_rec, rec_rows):
    blocks, most = members_ref.shape
    padded[...] = jnp.full(padded.shape, -1, i32)
    padded[:, :most] = members_ref[...]
    earlier = ones_where(iota((128, 128), 0) < iota((128, 128), 1)).astype(bf16)
    running = jnp.zeros((n_rec, 1), f32)
    out = []
    for b in range(blocks):
        ids = padded[b : b + 1, :]
        source = (lax.shift_right_arithmetic(ids, 7) * 171) >> 9
        row = ids - source * rec_rows
        source = jnp.where(ids >= 0, source, -1)
        hit = ones_where(iota((n_rec, 128), 0) == source)
        place = mm(hit.astype(bf16), earlier) + running
        running = running + jnp.sum(hit, axis=1, keepdims=True)
        out.append((source, row, hit, place))
    return out


def request_kernel(members_ref, out_ref, padded):
    n_rec = out_ref.shape[0]
    tables = bucket_tables(members_ref, padded, n_rec, LAN)
    lane = iota((n_rec, 128), 1)
    asked = jnp.zeros((n_rec, 128), f32)
    for k in range(CAP):
        found = jnp.zeros((n_rec, 128), f32)
        for source, row, hit, place in tables:
            found = found + jnp.where(place == k, hit, 0.0) * (row + 1).astype(f32)
        asked = jnp.where(lane == k, jnp.sum(found, axis=1, keepdims=True), asked)
    out_ref[...] = asked.astype(i32).reshape(out_ref.shape)


def wanted_rows(asked_ref):
    n_rec = asked_ref.shape[0]
    asked = asked_ref[...].reshape(n_rec, 1, 128).astype(f32)
    step = iota((n_rec, 2 * CAP, 128), 1)
    step = jnp.where(step >= CAP, step - CAP, step)
    mine = jnp.where(iota((n_rec, 2 * CAP, 128), 2) == step, asked, 0.0)
    wanted = jnp.sum(mine, axis=2, keepdims=True).astype(i32) - 1
    later = iota((n_rec, 2 * CAP, 1), 1) >= CAP
    return wanted + jnp.where(later & (wanted >= 0), LAN, 0)


def stack_kernel(emb_ref, out_ref):
    rows, width = emb_ref.shape
    out_ref[:rows, :] = emb_ref[:, : width // 2].astype(bf16)
    out_ref[rows:, :] = emb_ref[:, width // 2 :].astype(bf16)


def fetch_kernel(asked_ref, stacked_ref, out_hbm, out_s, sems):
    n_rec = asked_ref.shape[0]
    parts = sems.shape[0]
    rows = n_rec * 2 * CAP // parts
    wanted = wanted_rows(asked_ref)
    stores = []
    for t in range(parts):
        mine = wanted[t * n_rec // parts : (t + 1) * n_rec // parts]
        pick = ones_where(iota((n_rec // parts, 2 * CAP, 2 * LAN), 2) == mine).reshape(rows, 2 * LAN).astype(bf16)
        here = pl.ds(t * rows, rows)
        out_s[here, :] = mm(pick, stacked_ref[...]).astype(bf16)
        stores.append(pltpu.make_async_copy(out_s.at[here], out_hbm.at[here], sems.at[t]))
        stores[t].start()
    for store in stores:
        store.wait()


def prepare_kernel(
    members_ref, pairs_ref, labels_ref, asked_ref,
    gather_ref, table_ref, back_ref, padded,
):
    arrivals = gather_ref.shape[1]
    n_rec = arrivals // (2 * CAP)
    blocks, most = members_ref.shape
    tables = bucket_tables(members_ref, padded, n_rec, LAN)
    sub = iota((LAN, 128), 0)
    lane = iota((1, 128), 1)
    offset = jnp.zeros((1, 1), i32)
    offsets, lengths = [], []
    bucket = jnp.zeros((LAN, 1), f32)
    for b, (source, row, hit, place) in enumerate(tables):
        live = source >= 0
        length = jnp.sum(ones_where(live), axis=1, keepdims=True).astype(i32)
        offsets.append(offset)
        lengths.append(length)
        slot = jnp.where(live, offset + lane, -1)
        offset = offset + length
        at = jnp.sum(hit * place, axis=0, keepdims=True) + (source * (2 * CAP) + 1).astype(f32)
        bucket = bucket + jnp.sum(jnp.where(sub == slot, at, 0.0), axis=1, keepdims=True)
    bucket_col = bucket.astype(i32) - 1
    bucket_col = jnp.where(bucket_col < 0, -4096, bucket_col)
    bucket_row = jnp.transpose(jnp.broadcast_to(bucket, (LAN, 128)))[0:1, :].astype(i32) - 1
    bucket_row = jnp.where(bucket_row < 0, -4096, bucket_row)
    lanes = iota((SUB, arrivals), 1)
    gather_ref[:SUB, :] = ones_where(lanes == bucket_col[:SUB]).astype(bf16)
    gather_ref[SUB:, :] = ones_where(lanes == bucket_col[:SUB] + CAP).astype(bf16)
    rows = iota((arrivals, LAN), 0)
    table_ref[:arrivals, :LAN] = ones_where(rows == bucket_row).astype(bf16)
    table_ref[:arrivals, LAN:] = ones_where(rows == bucket_row + CAP).astype(bf16)

    col, row = iota((SUB, 1), 0), iota((1, LAN), 1)
    block_col, block_row = jnp.zeros((SUB, 1), i32), jnp.zeros((1, LAN), i32)
    count = jnp.zeros((1, LAN), f32) + lengths[0].astype(f32)
    for b in range(1, blocks):
        block_col = jnp.where(col >= offsets[b], b, block_col)
        block_row = jnp.where(row >= offsets[b], b, block_row)
        count = jnp.where(row >= offsets[b], lengths[b].astype(f32), count)
    block_col = jnp.where(col < LIVE, block_col, -1)
    block_row = jnp.where(row < LIVE, block_row, -2)
    counts = jnp.where((block_col == block_row) & (col != row), count, 0.0)
    table_ref[arrivals : arrivals + SUB, :LAN] = counts.astype(bf16)

    def packed(slots):
        at = jnp.zeros((1, 128), i32) + offsets[0]
        first = jnp.zeros((1, 128), i32)
        for b in range(1, blocks):
            at = jnp.where(slots >= b * most, offsets[b], at)
            first = jnp.where(slots >= b * most, b * most, first)
        return at + slots - first

    label = labels_ref[...].astype(f32)
    one = jnp.where(iota((SUB, 128), 0) == packed(pairs_ref[0:1, :]), 1.0, 0.0)
    two = ones_where(iota((LAN, 128), 0) == packed(pairs_ref[1:2, :])).astype(bf16)
    table_ref[arrivals : arrivals + SUB, LAN:] = nt((one * (1.0 - label)).astype(bf16), two).astype(bf16)
    table_ref[arrivals + SUB :, :LAN] = nt((one * label).astype(bf16), two).astype(bf16)
    table_ref[arrivals + SUB :, LAN:] = jnp.zeros((SUB, LAN), bf16)
    wanted = wanted_rows(asked_ref).reshape(arrivals, 1).astype(f32)
    wanted = jnp.transpose(jnp.broadcast_to(wanted, (arrivals, 128)))[0:1, :].astype(i32)
    back_ref[...] = ones_where(iota((2 * LAN, arrivals), 0) == wanted).astype(bf16)


def owner_kernel(
    arrived_ref, gather_hbm, weight_hbm, table_hbm,
    out_hbm, rows_ref, dscore_ref,
    gather_s, rows_s, right_s, stacked_s, weight_s, spread_s, terms_s, out_s, sems, out_sems,
):
    arrivals, half = arrived_ref.shape
    width = 2 * half
    terms_hbm, spread_hbm = table_hbm.at[arrivals:], table_hbm.at[:arrivals]
    loads = []
    for n, (source, target) in enumerate([
        (gather_hbm.at[:SUB], gather_s.at[:SUB]),
        (gather_hbm.at[SUB:], gather_s.at[SUB:]),
        (weight_hbm, weight_s),
        (terms_hbm, terms_s),
        (spread_hbm, spread_s),
    ]):
        loads.append(pltpu.make_async_copy(source, target, sems.at[n]))
        loads[n].start()
    loads[0].wait()
    rows_s[:SUB, :half] = mm(gather_s[:SUB, :], arrived_ref[...]).astype(bf16)
    loads[1].wait()
    rows_s[:SUB, half:] = mm(gather_s[SUB:, :], arrived_ref[...]).astype(bf16)
    rows_s[SUB:, :] = jnp.zeros((LAN - SUB, width), bf16)
    rows = rows_s[:SUB, :]
    rows_ref[...] = rows
    loads[2].wait()
    left = mm(rows, weight_s[...]).astype(bf16)
    right_s[:SUB, :] = nt(rows, weight_s[...]).astype(bf16)
    right_s[SUB:, :] = jnp.zeros((LAN - SUB, width), bf16)
    shifted = nt(left, rows_s[...]) - MARGIN
    small = jnp.exp(-jnp.abs(shifted))
    larger = 1.0 / (1.0 + small)
    smaller = small * larger
    up = jnp.where(shifted >= 0, larger, smaller)
    down = jnp.where(shifted >= 0, smaller, larger)
    loads[3].wait()
    count = terms_s[:SUB, :LAN].astype(f32)
    plus = terms_s[:SUB, LAN:].astype(f32)
    minus = terms_s[SUB:, :LAN].astype(f32)
    dscore = jnp.where(count > 0, up / jnp.maximum(count, 1.0), 0.0) + (up * plus - down * minus)
    dscore = dscore.astype(bf16)
    dscore_ref[...] = dscore
    grad = mm(dscore, right_s[...]) + tn(dscore, left)[:SUB]
    grad = grad.astype(bf16)
    stacked_s[:SUB, :] = grad[:, :half]
    stacked_s[SUB:LAN, :] = jnp.zeros((LAN - SUB, half), bf16)
    stacked_s[LAN : LAN + SUB, :] = grad[:, half:]
    stacked_s[LAN + SUB :, :] = jnp.zeros((LAN - SUB, half), bf16)
    loads[4].wait()
    parts = out_sems.shape[0]
    size = arrivals // parts
    stores = []
    for t in range(parts):
        here = pl.ds(t * size, size)
        out_s[here, :] = mm(spread_s[here, :], stacked_s[...]).astype(bf16)
        stores.append(pltpu.make_async_copy(out_s.at[here], out_hbm.at[here], out_sems.at[t]))
        stores[t].start()
    for store in stores:
        store.wait()


def weight_kernel(core_ref, rows_ref, dscore_ref, out_ref, rows_s):
    width = rows_ref.shape[1]
    rows_s[:SUB, :] = rows_ref[...]
    rows_s[SUB:, :] = jnp.zeros((LAN - SUB, width), bf16)
    carried = mm(dscore_ref[...], rows_s[...]).astype(bf16)
    core = core_ref[0]
    tile = 256
    for t in range(width // tile):
        part = tn(rows_s[:SUB, t * tile : (t + 1) * tile], carried)
        part = part.reshape(tile // 32, 2, 16, width)
        even = jnp.broadcast_to(core, (tile // 32, 16, width)) == 0
        part = jnp.where(even, part[:, 0], part[:, 1]).reshape(tile // 2, width)
        out_ref[t * tile // 2 : (t + 1) * tile // 2, :] = part.astype(out_ref.dtype)


def split_kernel(y_ref, keep_ref, got_ref, own_ref, *send_refs):
    size = own_ref.shape[1]
    for k in range(NY):
        at = pl.multiple_of(((y_ref[0] + k) % NY) * size, size)
        part = keep_ref[:, pl.ds(at, size)] + got_ref[:, pl.ds(at, size)].astype(f32)
        if k == 0:
            own_ref[...] = part
        else:
            send_refs[k - 1][...] = part.astype(bf16)


def join_kernel(y_ref, *refs):
    *piece_refs, out_ref = refs
    size = piece_refs[0].shape[1]
    for k, piece_ref in enumerate(piece_refs):
        at = pl.multiple_of(((y_ref[0] + NY - k) % NY) * size, size)
        out_ref[:, pl.ds(at, size)] = piece_ref[...]


def return_kernel(back_ref, pick_hbm, out_ref, pick_s, sem):
    half = back_ref.shape[1]
    load = pltpu.make_async_copy(pick_hbm, pick_s, sem)
    load.start()
    load.wait()
    total = mm(pick_s[...], back_ref[...])
    rec_rows = out_ref.shape[0]
    out_ref[:, :half] = total[:rec_rows]
    out_ref[:, half:] = total[rec_rows:]


def vmem(n):
    return [pl.BlockSpec(memory_space=pltpu.VMEM)] * n


def call(kernel, outs, n_in, scratch=(), flops=0, moved=0, smem=0, hbm=0, hbm_outs=0, grant=60):
    single = not isinstance(outs, (list, tuple))
    n_out = 1 if single else len(outs)
    out_specs = [pl.BlockSpec(memory_space=pltpu.HBM)] * hbm_outs + vmem(n_out - hbm_outs)
    return pl.pallas_call(
        kernel,
        out_shape=outs,
        in_specs=[pl.BlockSpec(memory_space=pltpu.SMEM)] * smem + vmem(n_in) + [pl.BlockSpec(memory_space=pltpu.HBM)] * hbm,
        out_specs=out_specs[0] if single else out_specs,
        scratch_shapes=list(scratch),
        compiler_params=pltpu.CompilerParams(vmem_limit_bytes=int(grant * MIB)),
        cost_estimate=pl.CostEstimate(flops=flops, bytes_accessed=moved, transcendentals=0),
    )


def shifted_blocks(value, axis, size):
    here = lax.axis_index(axis)
    got = []
    for k in range(1, size):
        block = lax.dynamic_index_in_dim(value, (here + k) % size, 0, keepdims=False).astype(bf16)
        got.append(lax.ppermute(block, axis, [(i, (i + k) % size) for i in range(size)]))
    total = lax.dynamic_index_in_dim(value, here, 0, keepdims=False)
    for block in got:
        total = total + block.astype(f32)
    return total


def on_device(embeddings, weight, members, pair_slots, labels):
    n_rec = NX * NZ * NC
    rec_rows, width = embeddings.shape[1:]
    half = width // 2
    arrivals = n_rec * 2 * CAP
    struct = jax.ShapeDtypeStruct
    ids = members[0]
    padded = pltpu.VMEM((ids.shape[0], 128), i32)

    requests = call(request_kernel, struct((n_rec, 1, 128), i32), 1, [padded], grant=16)(ids)
    asked = lax.all_to_all(requests, REC, split_axis=0, concat_axis=0, tiled=True)
    dma = pltpu.SemaphoreType.DMA
    stacked = call(
        stack_kernel, struct((2 * rec_rows, half), bf16), 1, flops=10**6, moved=3 * MIB, grant=16
    )(embeddings[0])
    found = call(
        fetch_kernel, struct((arrivals, half), bf16), 2,
        [pltpu.VMEM((arrivals, half), bf16), dma((4,))],
        flops=4 * arrivals * rec_rows * half, moved=3 * MIB, hbm_outs=1, grant=32,
    )(asked, stacked)
    arrived = lax.all_to_all(
        found.reshape(n_rec, 2 * CAP, half), REC, split_axis=0, concat_axis=0, tiled=True
    ).reshape(arrivals, half)
    gather, table, back = call(
        prepare_kernel,
        [
            struct((2 * SUB, arrivals), bf16),
            struct((arrivals + 2 * SUB, 2 * LAN), bf16),
            struct((2 * LAN, arrivals), bf16),
        ],
        4, [padded], moved=8 * MIB,
    )(ids, pair_slots[0].T, labels, asked)

    out, rows, dscore = call(
        owner_kernel,
        [struct((arrivals, half), bf16), struct((SUB, width), bf16), struct((SUB, LAN), bf16)],
        1,
        [pltpu.VMEM((2 * SUB, arrivals), bf16)]
        + [pltpu.VMEM((LAN, width), bf16)] * 2
        + [pltpu.VMEM((2 * LAN, half), bf16), pltpu.VMEM((width, width), bf16), pltpu.VMEM((arrivals, 2 * LAN), bf16)]
        + [pltpu.VMEM((2 * SUB, 2 * LAN), bf16), pltpu.VMEM((arrivals, half), bf16)]
        + [dma((5,)), dma((4,))],
        flops=4 * 10**9, moved=12 * MIB, hbm=3, hbm_outs=1, grant=49.5,
    )(arrived, gather, weight, table)
    returned = lax.all_to_all(
        out.reshape(n_rec, 2 * CAP, half), REC, split_axis=0, concat_axis=0, tiled=True
    ).reshape(arrivals, half)

    core = lax.axis_index("c").astype(i32).reshape(1)
    rows_core = width // NC

    def term(half_of, dtype):
        return call(
            weight_kernel, struct((rows_core, width), dtype), 2, [pltpu.VMEM((LAN, width), bf16)],
            flops=10**9, moved=4 * MIB, smem=1, grant=24,
        )(half_of, rows, dscore)

    send, keep = term(1 - core, bf16), term(core, f32)
    got = lax.ppermute(send, "c", [(0, 1), (1, 0)])
    y = lax.axis_index("y").astype(i32).reshape(1)
    cols = width // NY
    summed, *sends = call(
        split_kernel,
        [struct((rows_core, cols), f32)] + [struct((rows_core, cols), bf16)] * (NY - 1), 2,
        flops=10**6, moved=4 * MIB, smem=1, grant=24,
    )(y, keep, got)
    for k in range(1, NY):
        summed = summed + lax.ppermute(sends[k - 1], "y", [(i, (i + k) % NY) for i in range(NY)]).astype(f32)
    summed = shifted_blocks(summed.reshape(NX, NZ * 16, cols), "x", NX)
    shares = summed.reshape(NZ, 16, cols).astype(bf16)
    returned, shares = lax.optimization_barrier((returned, shares))
    shares = lax.all_to_all(shares, "z", split_axis=0, concat_axis=0, tiled=True)
    summed = jnp.sum(shares.astype(f32), axis=0)
    pieces = [summed]
    for k in range(1, NY):
        pieces.append(lax.ppermute(summed, "y", [(i, (i + k) % NY) for i in range(NY)]))
    emb_grad = call(
        return_kernel, struct((rec_rows, width), f32), 1, [pltpu.VMEM((2 * rec_rows, arrivals), bf16), dma],
        flops=4 * arrivals * rec_rows * half, moved=6 * MIB, hbm=1, grant=52,
    )(returned, back)
    weight_part = call(join_kernel, struct((16, width), f32), NY, smem=1, flops=10**4, moved=10**5, grant=16)(y, *pieces)
    return (emb_grad[None], weight_part)


def solution(mesh):
    fine = Mesh(mesh.devices.reshape(NX, NZ, NC, NY), ("x", "z", "c", "y"))
    return jax.shard_map(
        on_device,
        mesh=fine,
        in_specs=(
            P("y", REC, None),
            P(),
            P("y", REC, None),
            P("y", REC, None),
            P("y", REC),
        ),
        out_specs=(P("y", REC, None), P(REC, None)),
        check_vma=False,
    )
```

```python
import jax
import jax.numpy as jnp
from jax import lax
from jax.experimental import pallas as pl
from jax.experimental.pallas import tpu as pltpu
from jax.sharding import Mesh, PartitionSpec as P

f32, bf16, i32 = jnp.float32, jnp.bfloat16, jnp.int32

CAP = 12
LIVE = 264
SUB = 272
LAN = 384
MARGIN = 0.5
NX, NZ, NC, NY = 4, 8, 2, 4
REC = ("x", "z", "c")
MIB = 2**20


def iota(shape, dim):
    return lax.broadcasted_iota(i32, shape, dim)


def ones_where(mask):
    return jnp.where(mask, 1.0, 0.0).astype(f32)


def nt(a, b):
    return lax.dot_general(a, b, (((1,), (1,)), ((), ())), preferred_element_type=f32)


def tn(a, b):
    return lax.dot_general(a, b, (((0,), (0,)), ((), ())), preferred_element_type=f32)


def mm(a, b):
    return jnp.dot(a, b, preferred_element_type=f32)


def bucket_tables(members_ref, padded, n_rec, rec_rows):
    blocks, most = members_ref.shape
    padded[...] = jnp.full(padded.shape, -1, i32)
    padded[:, :most] = members_ref[...]
    earlier = ones_where(iota((128, 128), 0) < iota((128, 128), 1)).astype(bf16)
    running = jnp.zeros((n_rec, 1), f32)
    out = []
    for b in range(blocks):
        ids = padded[b : b + 1, :]
        source = (lax.shift_right_arithmetic(ids, 7) * 171) >> 9
        row = ids - source * rec_rows
        source = jnp.where(ids >= 0, source, -1)
        hit = ones_where(iota((n_rec, 128), 0) == source)
        place = mm(hit.astype(bf16), earlier) + running
        running = running + jnp.sum(hit, axis=1, keepdims=True)
        out.append((source, row, hit, place))
    return out


def request_kernel(members_ref, out_ref, padded):
    n_rec = out_ref.shape[0]
    tables = bucket_tables(members_ref, padded, n_rec, LAN)
    lane = iota((n_rec, 128), 1)
    asked = jnp.zeros((n_rec, 128), f32)
    for k in range(CAP):
        found = jnp.zeros((n_rec, 128), f32)
        for source, row, hit, place in tables:
            found = found + jnp.where(place == k, hit, 0.0) * (row + 1).astype(f32)
        asked = jnp.where(lane == k, jnp.sum(found, axis=1, keepdims=True), asked)
    out_ref[...] = asked.astype(i32).reshape(out_ref.shape)


def wanted_rows(asked_ref):
    n_rec = asked_ref.shape[0]
    asked = asked_ref[...].reshape(n_rec, 1, 128).astype(f32)
    step = iota((n_rec, 2 * CAP, 128), 1)
    step = jnp.where(step >= CAP, step - CAP, step)
    mine = jnp.where(iota((n_rec, 2 * CAP, 128), 2) == step, asked, 0.0)
    wanted = jnp.sum(mine, axis=2, keepdims=True).astype(i32) - 1
    later = iota((n_rec, 2 * CAP, 1), 1) >= CAP
    return wanted + jnp.where(later & (wanted >= 0), LAN, 0)


def stack_kernel(emb_ref, out_ref):
    rows, width = emb_ref.shape
    out_ref[:rows, :] = emb_ref[:, : width // 2].astype(bf16)
    out_ref[rows:, :] = emb_ref[:, width // 2 :].astype(bf16)


def fetch_kernel(asked_ref, stacked_ref, out_hbm, out_s, sems):
    n_rec = asked_ref.shape[0]
    parts = sems.shape[0]
    rows = n_rec * 2 * CAP // parts
    wanted = wanted_rows(asked_ref)
    stores = []
    for t in range(parts):
        mine = wanted[t * n_rec // parts : (t + 1) * n_rec // parts]
        pick = ones_where(iota((n_rec // parts, 2 * CAP, 2 * LAN), 2) == mine).reshape(rows, 2 * LAN).astype(bf16)
        here = pl.ds(t * rows, rows)
        out_s[here, :] = mm(pick, stacked_ref[...]).astype(bf16)
        stores.append(pltpu.make_async_copy(out_s.at[here], out_hbm.at[here], sems.at[t]))
        stores[t].start()
    for store in stores:
        store.wait()


def prepare_kernel(
    members_ref, pairs_ref, labels_ref, asked_ref,
    gather_ref, table_ref, back_ref, padded,
):
    arrivals = gather_ref.shape[1]
    n_rec = arrivals // (2 * CAP)
    blocks, most = members_ref.shape
    tables = bucket_tables(members_ref, padded, n_rec, LAN)
    sub = iota((LAN, 128), 0)
    lane = iota((1, 128), 1)
    offset = jnp.zeros((1, 1), i32)
    offsets, lengths = [], []
    bucket = jnp.zeros((LAN, 1), f32)
    for b, (source, row, hit, place) in enumerate(tables):
        live = source >= 0
        length = jnp.sum(ones_where(live), axis=1, keepdims=True).astype(i32)
        offsets.append(offset)
        lengths.append(length)
        slot = jnp.where(live, offset + lane, -1)
        offset = offset + length
        at = jnp.sum(hit * place, axis=0, keepdims=True) + (source * (2 * CAP) + 1).astype(f32)
        bucket = bucket + jnp.sum(jnp.where(sub == slot, at, 0.0), axis=1, keepdims=True)
    bucket_col = bucket.astype(i32) - 1
    bucket_col = jnp.where(bucket_col < 0, -4096, bucket_col)
    bucket_row = jnp.transpose(jnp.broadcast_to(bucket, (LAN, 128)))[0:1, :].astype(i32) - 1
    bucket_row = jnp.where(bucket_row < 0, -4096, bucket_row)
    lanes = iota((SUB, arrivals), 1)
    gather_ref[:SUB, :] = ones_where(lanes == bucket_col[:SUB]).astype(bf16)
    gather_ref[SUB:, :] = ones_where(lanes == bucket_col[:SUB] + CAP).astype(bf16)
    rows = iota((arrivals, LAN), 0)
    table_ref[:arrivals, :LAN] = ones_where(rows == bucket_row).astype(bf16)
    table_ref[:arrivals, LAN:] = ones_where(rows == bucket_row + CAP).astype(bf16)

    col, row = iota((SUB, 1), 0), iota((1, LAN), 1)
    block_col, block_row = jnp.zeros((SUB, 1), i32), jnp.zeros((1, LAN), i32)
    count = jnp.zeros((1, LAN), f32) + lengths[0].astype(f32)
    for b in range(1, blocks):
        block_col = jnp.where(col >= offsets[b], b, block_col)
        block_row = jnp.where(row >= offsets[b], b, block_row)
        count = jnp.where(row >= offsets[b], lengths[b].astype(f32), count)
    block_col = jnp.where(col < LIVE, block_col, -1)
    block_row = jnp.where(row < LIVE, block_row, -2)
    counts = jnp.where((block_col == block_row) & (col != row), count, 0.0)
    table_ref[arrivals : arrivals + SUB, :LAN] = counts.astype(bf16)

    def packed(slots):
        at = jnp.zeros((1, 128), i32) + offsets[0]
        first = jnp.zeros((1, 128), i32)
        for b in range(1, blocks):
            at = jnp.where(slots >= b * most, offsets[b], at)
            first = jnp.where(slots >= b * most, b * most, first)
        return at + slots - first

    label = labels_ref[...].astype(f32)
    one = jnp.where(iota((SUB, 128), 0) == packed(pairs_ref[0:1, :]), 1.0, 0.0)
    two = ones_where(iota((LAN, 128), 0) == packed(pairs_ref[1:2, :])).astype(bf16)
    table_ref[arrivals : arrivals + SUB, LAN:] = nt((one * (1.0 - label)).astype(bf16), two).astype(bf16)
    table_ref[arrivals + SUB :, :LAN] = nt((one * label).astype(bf16), two).astype(bf16)
    table_ref[arrivals + SUB :, LAN:] = jnp.zeros((SUB, LAN), bf16)
    wanted = wanted_rows(asked_ref).reshape(arrivals, 1).astype(f32)
    wanted = jnp.transpose(jnp.broadcast_to(wanted, (arrivals, 128)))[0:1, :].astype(i32)
    back_ref[...] = ones_where(iota((2 * LAN, arrivals), 0) == wanted).astype(bf16)


def owner_kernel(
    arrived_ref, gather_hbm, weight_hbm, table_hbm,
    out_hbm, rows_ref, dscore_ref,
    gather_s, rows_s, right_s, stacked_s, weight_s, spread_s, terms_s, out_s, sems, out_sems,
):
    arrivals, half = arrived_ref.shape
    width = 2 * half
    terms_hbm, spread_hbm = table_hbm.at[arrivals:], table_hbm.at[:arrivals]
    loads = []
    for n, (source, target) in enumerate([
        (gather_hbm.at[:SUB], gather_s.at[:SUB]),
        (gather_hbm.at[SUB:], gather_s.at[SUB:]),
        (weight_hbm, weight_s),
        (terms_hbm, terms_s),
        (spread_hbm, spread_s),
    ]):
        loads.append(pltpu.make_async_copy(source, target, sems.at[n]))
        loads[n].start()
    loads[0].wait()
    rows_s[:SUB, :half] = mm(gather_s[:SUB, :], arrived_ref[...]).astype(bf16)
    loads[1].wait()
    rows_s[:SUB, half:] = mm(gather_s[SUB:, :], arrived_ref[...]).astype(bf16)
    rows_s[SUB:, :] = jnp.zeros((LAN - SUB, width), bf16)
    rows = rows_s[:SUB, :]
    rows_ref[...] = rows
    loads[2].wait()
    left = mm(rows, weight_s[...]).astype(bf16)
    right_s[:SUB, :] = nt(rows, weight_s[...]).astype(bf16)
    right_s[SUB:, :] = jnp.zeros((LAN - SUB, width), bf16)
    shifted = nt(left, rows_s[...]) - MARGIN
    small = jnp.exp(-jnp.abs(shifted))
    larger = 1.0 / (1.0 + small)
    smaller = small * larger
    up = jnp.where(shifted >= 0, larger, smaller)
    down = jnp.where(shifted >= 0, smaller, larger)
    loads[3].wait()
    count = terms_s[:SUB, :LAN].astype(f32)
    plus = terms_s[:SUB, LAN:].astype(f32)
    minus = terms_s[SUB:, :LAN].astype(f32)
    dscore = jnp.where(count > 0, up / jnp.maximum(count, 1.0), 0.0) + (up * plus - down * minus)
    dscore = dscore.astype(bf16)
    dscore_ref[...] = dscore
    grad = mm(dscore, right_s[...]) + tn(dscore, left)[:SUB]
    grad = grad.astype(bf16)
    stacked_s[:SUB, :] = grad[:, :half]
    stacked_s[SUB:LAN, :] = jnp.zeros((LAN - SUB, half), bf16)
    stacked_s[LAN : LAN + SUB, :] = grad[:, half:]
    stacked_s[LAN + SUB :, :] = jnp.zeros((LAN - SUB, half), bf16)
    loads[4].wait()
    parts = out_sems.shape[0]
    size = arrivals // parts
    stores = []
    for t in range(parts):
        here = pl.ds(t * size, size)
        out_s[here, :] = mm(spread_s[here, :], stacked_s[...]).astype(bf16)
        stores.append(pltpu.make_async_copy(out_s.at[here], out_hbm.at[here], out_sems.at[t]))
        stores[t].start()
    for store in stores:
        store.wait()


def weight_kernel(core_ref, rows_ref, dscore_ref, out_ref, rows_s):
    width = rows_ref.shape[1]
    rows_s[:SUB, :] = rows_ref[...]
    rows_s[SUB:, :] = jnp.zeros((LAN - SUB, width), bf16)
    carried = mm(dscore_ref[...], rows_s[...]).astype(bf16)
    core = core_ref[0]
    tile = 256
    for t in range(width // tile):
        part = tn(rows_s[:SUB, t * tile : (t + 1) * tile], carried)
        part = part.reshape(tile // 32, 2, 16, width)
        even = jnp.broadcast_to(core, (tile // 32, 16, width)) == 0
        part = jnp.where(even, part[:, 0], part[:, 1]).reshape(tile // 2, width)
        out_ref[t * tile // 2 : (t + 1) * tile // 2, :] = part.astype(out_ref.dtype)


def split_kernel(y_ref, keep_ref, got_ref, own_ref, *send_refs):
    size = own_ref.shape[1]
    for k in range(NY):
        at = pl.multiple_of(((y_ref[0] + k) % NY) * size, size)
        part = keep_ref[:, pl.ds(at, size)] + got_ref[:, pl.ds(at, size)].astype(f32)
        if k == 0:
            own_ref[...] = part
        else:
            send_refs[k - 1][...] = part.astype(bf16)


def join_kernel(y_ref, *refs):
    *piece_refs, out_ref = refs
    size = piece_refs[0].shape[1]
    for k, piece_ref in enumerate(piece_refs):
        at = pl.multiple_of(((y_ref[0] + NY - k) % NY) * size, size)
        out_ref[:, pl.ds(at, size)] = piece_ref[...]


def return_kernel(back_ref, pick_hbm, out_hbm, pick_s, out_s, in_sems, out_sems):
    half = back_ref.shape[1]
    rows = out_s.shape[0]
    loads = [
        pltpu.make_async_copy(pick_hbm.at[pl.ds(h * rows, rows)], pick_s.at[pl.ds(h * rows, rows)], in_sems.at[h])
        for h in range(2)
    ]
    stores = [
        pltpu.make_async_copy(
            out_s.at[:, pl.ds(h * half, half)], out_hbm.at[:, pl.ds(h * half, half)], out_sems.at[h]
        )
        for h in range(2)
    ]
    for load in loads:
        load.start()
    for h in range(2):
        loads[h].wait()
        out_s[:, h * half : (h + 1) * half] = mm(pick_s[h * rows : (h + 1) * rows, :], back_ref[...])
        stores[h].start()
    for store in stores:
        store.wait()


def vmem(n):
    return [pl.BlockSpec(memory_space=pltpu.VMEM)] * n


def call(kernel, outs, n_in, scratch=(), flops=0, moved=0, smem=0, hbm=0, hbm_outs=0, grant=60):
    single = not isinstance(outs, (list, tuple))
    n_out = 1 if single else len(outs)
    out_specs = [pl.BlockSpec(memory_space=pltpu.HBM)] * hbm_outs + vmem(n_out - hbm_outs)
    return pl.pallas_call(
        kernel,
        out_shape=outs,
        in_specs=[pl.BlockSpec(memory_space=pltpu.SMEM)] * smem + vmem(n_in) + [pl.BlockSpec(memory_space=pltpu.HBM)] * hbm,
        out_specs=out_specs[0] if single else out_specs,
        scratch_shapes=list(scratch),
        compiler_params=pltpu.CompilerParams(vmem_limit_bytes=int(grant * MIB)),
        cost_estimate=pl.CostEstimate(flops=flops, bytes_accessed=moved, transcendentals=0),
    )


def shifted_blocks(value, axis, size):
    here = lax.axis_index(axis)
    got = []
    for k in (2, 1, 3):
        block = lax.dynamic_index_in_dim(value, (here + k) % size, 0, keepdims=False).astype(bf16)
        got.append(lax.ppermute(block, axis, [(i, (i + k) % size) for i in range(size)]))
    total = lax.dynamic_index_in_dim(value, here, 0, keepdims=False)
    for block in got:
        total = total + block.astype(f32)
    return total


def on_device(embeddings, weight, members, pair_slots, labels):
    n_rec = NX * NZ * NC
    rec_rows, width = embeddings.shape[1:]
    half = width // 2
    arrivals = n_rec * 2 * CAP
    struct = jax.ShapeDtypeStruct
    ids = members[0]
    padded = pltpu.VMEM((ids.shape[0], 128), i32)

    requests = call(request_kernel, struct((n_rec, 1, 128), i32), 1, [padded], grant=16)(ids)
    asked = lax.all_to_all(requests, REC, split_axis=0, concat_axis=0, tiled=True)
    dma = pltpu.SemaphoreType.DMA
    stacked = call(
        stack_kernel, struct((2 * rec_rows, half), bf16), 1, flops=10**6, moved=3 * MIB, grant=16
    )(embeddings[0])
    found = call(
        fetch_kernel, struct((arrivals, half), bf16), 2,
        [pltpu.VMEM((arrivals, half), bf16), dma((4,))],
        flops=4 * arrivals * rec_rows * half, moved=3 * MIB, hbm_outs=1, grant=32,
    )(asked, stacked)
    arrived = lax.all_to_all(
        found.reshape(n_rec, 2 * CAP, half), REC, split_axis=0, concat_axis=0, tiled=True
    ).reshape(arrivals, half)
    gather, table, back = call(
        prepare_kernel,
        [
            struct((2 * SUB, arrivals), bf16),
            struct((arrivals + 2 * SUB, 2 * LAN), bf16),
            struct((2 * LAN, arrivals), bf16),
        ],
        4, [padded], moved=8 * MIB,
    )(ids, pair_slots[0].T, labels, asked)

    out, rows, dscore = call(
        owner_kernel,
        [struct((arrivals, half), bf16), struct((SUB, width), bf16), struct((SUB, LAN), bf16)],
        1,
        [pltpu.VMEM((2 * SUB, arrivals), bf16)]
        + [pltpu.VMEM((LAN, width), bf16)] * 2
        + [pltpu.VMEM((2 * LAN, half), bf16), pltpu.VMEM((width, width), bf16), pltpu.VMEM((arrivals, 2 * LAN), bf16)]
        + [pltpu.VMEM((2 * SUB, 2 * LAN), bf16), pltpu.VMEM((arrivals, half), bf16)]
        + [dma((5,)), dma((4,))],
        flops=4 * 10**9, moved=12 * MIB, hbm=3, hbm_outs=1, grant=49.5,
    )(arrived, gather, weight, table)
    returned = lax.all_to_all(
        out.reshape(n_rec, 2 * CAP, half), REC, split_axis=0, concat_axis=0, tiled=True
    ).reshape(arrivals, half)

    core = lax.axis_index("c").astype(i32).reshape(1)
    rows_core = width // NC

    def term(half_of, dtype):
        return call(
            weight_kernel, struct((rows_core, width), dtype), 2, [pltpu.VMEM((LAN, width), bf16)],
            flops=10**9, moved=4 * MIB, smem=1, grant=24,
        )(half_of, rows, dscore)

    send, keep = term(1 - core, bf16), term(core, f32)
    got = lax.ppermute(send, "c", [(0, 1), (1, 0)])
    y = lax.axis_index("y").astype(i32).reshape(1)
    cols = width // NY
    summed, *sends = call(
        split_kernel,
        [struct((rows_core, cols), f32)] + [struct((rows_core, cols), bf16)] * (NY - 1), 2,
        flops=10**6, moved=4 * MIB, smem=1, grant=24,
    )(y, keep, got)
    for k in (2, 1, 3):
        summed = summed + lax.ppermute(sends[k - 1], "y", [(i, (i + k) % NY) for i in range(NY)]).astype(f32)
    summed = shifted_blocks(summed.reshape(NX, NZ * 16, cols), "x", NX)
    half_z = NZ // 2
    z = lax.axis_index("z")
    summed = summed.reshape(2, half_z, 16, cols)
    far = lax.dynamic_index_in_dim(summed, 1 - z // half_z, 0, keepdims=False).astype(bf16)
    near = lax.dynamic_index_in_dim(summed, z // half_z, 0, keepdims=False)
    far = lax.ppermute(far, "z", [(i, (i + half_z) % NZ) for i in range(NZ)])
    emb_grad = call(
        return_kernel, struct((rec_rows, width), f32), 1,
        [pltpu.VMEM((2 * rec_rows, arrivals), bf16), pltpu.VMEM((rec_rows, width), f32), dma((2,)), dma((2,))],
        flops=4 * arrivals * rec_rows * half, moved=6 * MIB, hbm=1, hbm_outs=1, grant=52,
    )(returned, back)
    emb_grad, far = lax.optimization_barrier((emb_grad, far))
    summed = near + far.astype(f32)
    blocks = []
    for k in range(1, half_z):
        block = lax.dynamic_index_in_dim(summed, (z + k) % half_z, 0, keepdims=False).astype(bf16)
        to = [(i, i // half_z * half_z + (i + k) % half_z) for i in range(NZ)]
        blocks.append(lax.ppermute(block, "z", to))
    summed = lax.dynamic_index_in_dim(summed, z % half_z, 0, keepdims=False)
    for block in blocks:
        summed = summed + block.astype(f32)
    pieces = [summed]
    for k in range(1, NY):
        pieces.append(lax.ppermute(summed, "y", [(i, (i + k) % NY) for i in range(NY)]))
    weight_part = call(join_kernel, struct((16, width), f32), NY, smem=1, flops=10**4, moved=10**5, grant=16)(y, *pieces)
    return (emb_grad[None], weight_part)


def solution(mesh):
    fine = Mesh(mesh.devices.reshape(NX, NZ, NC, NY), ("x", "z", "c", "y"))
    return jax.shard_map(
        on_device,
        mesh=fine,
        in_specs=(
            P("y", REC, None),
            P(),
            P("y", REC, None),
            P("y", REC, None),
            P("y", REC),
        ),
        out_specs=(P("y", REC, None), P(REC, None)),
        check_vma=False,
    )
```

```python
import jax
import jax.numpy as jnp
from jax import lax
from jax.experimental import pallas as pl
from jax.experimental.pallas import tpu as pltpu
from jax.sharding import Mesh, PartitionSpec as P

f32, bf16, i32 = jnp.float32, jnp.bfloat16, jnp.int32

CAP = 12
LIVE = 264
SUB = 272
LAN = 384
MARGIN = 0.5
NX, NZ, NC, NY = 4, 8, 2, 4
REC = ("x", "z", "c")
MIB = 2**20


def iota(shape, dim):
    return lax.broadcasted_iota(i32, shape, dim)


def ones_where(mask):
    return jnp.where(mask, 1.0, 0.0).astype(f32)


def nt(a, b):
    return lax.dot_general(a, b, (((1,), (1,)), ((), ())), preferred_element_type=f32)


def tn(a, b):
    return lax.dot_general(a, b, (((0,), (0,)), ((), ())), preferred_element_type=f32)


def mm(a, b):
    return jnp.dot(a, b, preferred_element_type=f32)


def bucket_tables(members_ref, padded, n_rec, rec_rows):
    blocks, most = members_ref.shape
    padded[...] = jnp.full(padded.shape, -1, i32)
    padded[:, :most] = members_ref[...]
    earlier = ones_where(iota((128, 128), 0) < iota((128, 128), 1)).astype(bf16)
    running = jnp.zeros((n_rec, 1), f32)
    out = []
    for b in range(blocks):
        ids = padded[b : b + 1, :]
        source = (lax.shift_right_arithmetic(ids, 7) * 171) >> 9
        row = ids - source * rec_rows
        source = jnp.where(ids >= 0, source, -1)
        hit = ones_where(iota((n_rec, 128), 0) == source)
        place = mm(hit.astype(bf16), earlier) + running
        running = running + jnp.sum(hit, axis=1, keepdims=True)
        out.append((source, row, hit, place))
    return out


def request_kernel(members_ref, out_ref, padded):
    n_rec = out_ref.shape[0]
    tables = bucket_tables(members_ref, padded, n_rec, LAN)
    lane = iota((n_rec, 128), 1)
    asked = jnp.zeros((n_rec, 128), f32)
    for k in range(CAP):
        found = jnp.zeros((n_rec, 128), f32)
        for source, row, hit, place in tables:
            found = found + jnp.where(place == k, hit, 0.0) * (row + 1).astype(f32)
        asked = jnp.where(lane == k, jnp.sum(found, axis=1, keepdims=True), asked)
    out_ref[...] = asked.astype(i32).reshape(out_ref.shape)


def wanted_rows(asked_ref):
    n_rec = asked_ref.shape[0]
    asked = asked_ref[...].reshape(n_rec, 1, 128).astype(f32)
    step = iota((n_rec, 2 * CAP, 128), 1)
    step = jnp.where(step >= CAP, step - CAP, step)
    mine = jnp.where(iota((n_rec, 2 * CAP, 128), 2) == step, asked, 0.0)
    wanted = jnp.sum(mine, axis=2, keepdims=True).astype(i32) - 1
    later = iota((n_rec, 2 * CAP, 1), 1) >= CAP
    return wanted + jnp.where(later & (wanted >= 0), LAN, 0)


def stack_kernel(emb_ref, out_ref):
    rows, width = emb_ref.shape
    out_ref[:rows, :] = emb_ref[:, : width // 2].astype(bf16)
    out_ref[rows:, :] = emb_ref[:, width // 2 :].astype(bf16)


def fetch_kernel(asked_ref, stacked_ref, out_hbm, out_s, sems):
    n_rec = asked_ref.shape[0]
    parts = sems.shape[0]
    rows = n_rec * 2 * CAP // parts
    wanted = wanted_rows(asked_ref)
    stores = []
    for t in range(parts):
        mine = wanted[t * n_rec // parts : (t + 1) * n_rec // parts]
        pick = ones_where(iota((n_rec // parts, 2 * CAP, 2 * LAN), 2) == mine).reshape(rows, 2 * LAN).astype(bf16)
        here = pl.ds(t * rows, rows)
        out_s[here, :] = mm(pick, stacked_ref[...]).astype(bf16)
        stores.append(pltpu.make_async_copy(out_s.at[here], out_hbm.at[here], sems.at[t]))
        stores[t].start()
    for store in stores:
        store.wait()


def prepare_kernel(
    members_ref, pairs_ref, labels_ref, asked_ref, weight_ref,
    gather_ref, table_ref, back_ref, turned_ref, padded,
):
    arrivals = gather_ref.shape[1]
    n_rec = arrivals // (2 * CAP)
    blocks, most = members_ref.shape
    tables = bucket_tables(members_ref, padded, n_rec, LAN)
    sub = iota((LAN, 128), 0)
    lane = iota((1, 128), 1)
    offset = jnp.zeros((1, 1), i32)
    offsets, lengths = [], []
    bucket = jnp.zeros((LAN, 1), f32)
    for b, (source, row, hit, place) in enumerate(tables):
        live = source >= 0
        length = jnp.sum(ones_where(live), axis=1, keepdims=True).astype(i32)
        offsets.append(offset)
        lengths.append(length)
        slot = jnp.where(live, offset + lane, -1)
        offset = offset + length
        at = jnp.sum(hit * place, axis=0, keepdims=True) + (source * (2 * CAP) + 1).astype(f32)
        bucket = bucket + jnp.sum(jnp.where(sub == slot, at, 0.0), axis=1, keepdims=True)
    bucket_col = bucket.astype(i32) - 1
    bucket_col = jnp.where(bucket_col < 0, -4096, bucket_col)
    bucket_row = jnp.transpose(jnp.broadcast_to(bucket, (LAN, 128)))[0:1, :].astype(i32) - 1
    bucket_row = jnp.where(bucket_row < 0, -4096, bucket_row)
    lanes = iota((SUB, arrivals), 1)
    gather_ref[:SUB, :] = ones_where(lanes == bucket_col[:SUB]).astype(bf16)
    gather_ref[SUB:, :] = ones_where(lanes == bucket_col[:SUB] + CAP).astype(bf16)
    rows = iota((arrivals, LAN), 0)
    table_ref[:arrivals, :LAN] = ones_where(rows == bucket_row).astype(bf16)
    table_ref[:arrivals, LAN:] = ones_where(rows == bucket_row + CAP).astype(bf16)

    col, row = iota((SUB, 1), 0), iota((1, LAN), 1)
    block_col, block_row = jnp.zeros((SUB, 1), i32), jnp.zeros((1, LAN), i32)
    count = jnp.zeros((1, LAN), f32) + lengths[0].astype(f32)
    for b in range(1, blocks):
        block_col = jnp.where(col >= offsets[b], b, block_col)
        block_row = jnp.where(row >= offsets[b], b, block_row)
        count = jnp.where(row >= offsets[b], lengths[b].astype(f32), count)
    block_col = jnp.where(col < LIVE, block_col, -1)
    block_row = jnp.where(row < LIVE, block_row, -2)
    counts = jnp.where((block_col == block_row) & (col != row), count, 0.0)
    table_ref[arrivals : arrivals + SUB, :LAN] = counts.astype(bf16)

    def packed(slots):
        at = jnp.zeros((1, 128), i32) + offsets[0]
        first = jnp.zeros((1, 128), i32)
        for b in range(1, blocks):
            at = jnp.where(slots >= b * most, offsets[b], at)
            first = jnp.where(slots >= b * most, b * most, first)
        return at + slots - first

    label = labels_ref[...].astype(f32)
    one = jnp.where(iota((SUB, 128), 0) == packed(pairs_ref[0:1, :]), 1.0, 0.0)
    two = ones_where(iota((LAN, 128), 0) == packed(pairs_ref[1:2, :])).astype(bf16)
    table_ref[arrivals : arrivals + SUB, LAN:] = nt((one * (1.0 - label)).astype(bf16), two).astype(bf16)
    table_ref[arrivals + SUB :, :LAN] = nt((one * label).astype(bf16), two).astype(bf16)
    table_ref[arrivals + SUB :, LAN:] = jnp.zeros((SUB, LAN), bf16)
    wanted = wanted_rows(asked_ref).reshape(arrivals, 1).astype(f32)
    wanted = jnp.transpose(jnp.broadcast_to(wanted, (arrivals, 128)))[0:1, :].astype(i32)
    back_ref[...] = ones_where(iota((2 * LAN, arrivals), 0) == wanted).astype(bf16)
    turned_ref[...] = jnp.transpose(weight_ref[...])


def owner_kernel(
    arrived_ref, gather_hbm, weight_hbm, turned_hbm, table_hbm,
    out_hbm, rows_ref, dscore_ref,
    gather_s, rows_s, right_s, stacked_s, weight_s, turned_s, spread_s, terms_s, out_s, sems, out_sems,
):
    arrivals, half = arrived_ref.shape
    width = 2 * half
    terms_hbm, spread_hbm = table_hbm.at[arrivals:], table_hbm.at[:arrivals]
    loads = []
    for n, (source, target) in enumerate([
        (gather_hbm.at[:SUB], gather_s.at[:SUB]),
        (gather_hbm.at[SUB:], gather_s.at[SUB:]),
        (weight_hbm, weight_s),
        (turned_hbm, turned_s),
        (terms_hbm, terms_s),
        (spread_hbm, spread_s),
    ]):
        loads.append(pltpu.make_async_copy(source, target, sems.at[n]))
        loads[n].start()
    loads[0].wait()
    rows_s[:SUB, :half] = mm(gather_s[:SUB, :], arrived_ref[...]).astype(bf16)
    loads[1].wait()
    rows_s[:SUB, half:] = mm(gather_s[SUB:, :], arrived_ref[...]).astype(bf16)
    rows_s[SUB:, :] = jnp.zeros((LAN - SUB, width), bf16)
    rows = rows_s[:SUB, :]
    rows_ref[...] = rows
    loads[2].wait()
    left = mm(rows, weight_s[...]).astype(bf16)
    loads[3].wait()
    right_s[:SUB, :] = mm(rows, turned_s[...]).astype(bf16)
    right_s[SUB:, :] = jnp.zeros((LAN - SUB, width), bf16)
    shifted = nt(left, rows_s[...]) - MARGIN
    small = jnp.exp(-jnp.abs(shifted))
    larger = 1.0 / (1.0 + small)
    smaller = small * larger
    up = jnp.where(shifted >= 0, larger, smaller)
    down = jnp.where(shifted >= 0, smaller, larger)
    loads[4].wait()
    count = terms_s[:SUB, :LAN].astype(f32)
    plus = terms_s[:SUB, LAN:].astype(f32)
    minus = terms_s[SUB:, :LAN].astype(f32)
    dscore = jnp.where(count > 0, up / jnp.maximum(count, 1.0), 0.0) + (up * plus - down * minus)
    dscore = dscore.astype(bf16)
    dscore_ref[...] = dscore
    grad = mm(dscore, right_s[...]) + tn(dscore, left)[:SUB]
    grad = grad.astype(bf16)
    stacked_s[:SUB, :] = grad[:, :half]
    stacked_s[SUB:LAN, :] = jnp.zeros((LAN - SUB, half), bf16)
    stacked_s[LAN : LAN + SUB, :] = grad[:, half:]
    stacked_s[LAN + SUB :, :] = jnp.zeros((LAN - SUB, half), bf16)
    loads[5].wait()
    parts = out_sems.shape[0]
    size = arrivals // parts
    stores = []
    for t in range(parts):
        here = pl.ds(t * size, size)
        out_s[here, :] = mm(spread_s[here, :], stacked_s[...]).astype(bf16)
        stores.append(pltpu.make_async_copy(out_s.at[here], out_hbm.at[here], out_sems.at[t]))
        stores[t].start()
    for store in stores:
        store.wait()


def half_term(core, rows_ref, dscore_ref, rows_s):
    width = rows_ref.shape[1]
    rows_s[:SUB, :] = rows_ref[...]
    rows_s[SUB:, :] = jnp.zeros((LAN - SUB, width), bf16)
    carried = mm(dscore_ref[...], rows_s[...]).astype(bf16)
    tile = 256
    for t in range(width // tile):
        part = tn(rows_s[:SUB, t * tile : (t + 1) * tile], carried)
        part = part.reshape(tile // 32, 2, 16, width)
        even = jnp.broadcast_to(core, (tile // 32, 16, width)) == 0
        yield pl.ds(t * tile // 2, tile // 2), jnp.where(even, part[:, 0], part[:, 1]).reshape(tile // 2, width)


def keep_kernel(core_ref, rows_ref, dscore_ref, out_ref, rows_s):
    for place, part in half_term(core_ref[0], rows_ref, dscore_ref, rows_s):
        out_ref[place, :] = part


def send_kernel(core_ref, rows_ref, dscore_ref, out_hbm, rows_s, out_s, sems):
    stores = []
    for n, (place, part) in enumerate(half_term(core_ref[0], rows_ref, dscore_ref, rows_s)):
        out_s[place, :] = part.astype(bf16)
        stores.append(pltpu.make_async_copy(out_s.at[place], out_hbm.at[place], sems.at[n]))
        stores[n].start()
    for store in stores:
        store.wait()


def split_kernel(y_ref, keep_ref, got_ref, own_ref, *send_refs):
    size = own_ref.shape[1]
    for k in range(NY):
        at = pl.multiple_of(((y_ref[0] + k) % NY) * size, size)
        part = keep_ref[:, pl.ds(at, size)] + got_ref[:, pl.ds(at, size)].astype(f32)
        if k == 0:
            own_ref[...] = part
        else:
            send_refs[k - 1][...] = part.astype(bf16)


def join_kernel(y_ref, *refs):
    *piece_refs, out_ref = refs
    size = piece_refs[0].shape[1]
    for k, piece_ref in enumerate(piece_refs):
        at = pl.multiple_of(((y_ref[0] + NY - k) % NY) * size, size)
        out_ref[:, pl.ds(at, size)] = piece_ref[...]


def return_kernel(back_ref, pick_hbm, out_hbm, pick_s, out_s, in_sems, out_sems):
    half = back_ref.shape[1]
    rows = out_s.shape[0]
    loads = [
        pltpu.make_async_copy(pick_hbm.at[pl.ds(h * rows, rows)], pick_s.at[pl.ds(h * rows, rows)], in_sems.at[h])
        for h in range(2)
    ]
    stores = [
        pltpu.make_async_copy(
            out_s.at[:, pl.ds(h * half, half)], out_hbm.at[:, pl.ds(h * half, half)], out_sems.at[h]
        )
        for h in range(2)
    ]
    for load in loads:
        load.start()
    for h in range(2):
        loads[h].wait()
        out_s[:, h * half : (h + 1) * half] = mm(pick_s[h * rows : (h + 1) * rows, :], back_ref[...])
        stores[h].start()
    for store in stores:
        store.wait()


def vmem(n):
    return [pl.BlockSpec(memory_space=pltpu.VMEM)] * n


def call(kernel, outs, n_in, scratch=(), flops=0, moved=0, smem=0, hbm=0, hbm_outs=0, grant=60):
    single = not isinstance(outs, (list, tuple))
    n_out = 1 if single else len(outs)
    out_specs = [pl.BlockSpec(memory_space=pltpu.HBM)] * hbm_outs + vmem(n_out - hbm_outs)
    return pl.pallas_call(
        kernel,
        out_shape=outs,
        in_specs=[pl.BlockSpec(memory_space=pltpu.SMEM)] * smem + vmem(n_in) + [pl.BlockSpec(memory_space=pltpu.HBM)] * hbm,
        out_specs=out_specs[0] if single else out_specs,
        scratch_shapes=list(scratch),
        compiler_params=pltpu.CompilerParams(vmem_limit_bytes=int(grant * MIB)),
        cost_estimate=pl.CostEstimate(flops=flops, bytes_accessed=moved, transcendentals=0),
    )


def shifted_blocks(value, axis, size):
    here = lax.axis_index(axis)
    got = []
    for k in (2, 1, 3):
        block = lax.dynamic_index_in_dim(value, (here + k) % size, 0, keepdims=False).astype(bf16)
        got.append(lax.ppermute(block, axis, [(i, (i + k) % size) for i in range(size)]))
    total = lax.dynamic_index_in_dim(value, here, 0, keepdims=False)
    for block in got:
        total = total + block.astype(f32)
    return total


def on_device(embeddings, weight, members, pair_slots, labels):
    n_rec = NX * NZ * NC
    rec_rows, width = embeddings.shape[1:]
    half = width // 2
    arrivals = n_rec * 2 * CAP
    struct = jax.ShapeDtypeStruct
    ids = members[0]
    padded = pltpu.VMEM((ids.shape[0], 128), i32)

    requests = call(request_kernel, struct((n_rec, 1, 128), i32), 1, [padded], grant=16)(ids)
    asked = lax.all_to_all(requests, REC, split_axis=0, concat_axis=0, tiled=True)
    dma = pltpu.SemaphoreType.DMA
    stacked = call(
        stack_kernel, struct((2 * rec_rows, half), bf16), 1, flops=10**6, moved=3 * MIB, grant=16
    )(embeddings[0])
    found = call(
        fetch_kernel, struct((arrivals, half), bf16), 2,
        [pltpu.VMEM((arrivals, half), bf16), dma((4,))],
        flops=4 * arrivals * rec_rows * half, moved=3 * MIB, hbm_outs=1, grant=32,
    )(asked, stacked)
    arrived = lax.all_to_all(
        found.reshape(n_rec, 2 * CAP, half), REC, split_axis=0, concat_axis=0, tiled=True
    ).reshape(arrivals, half)
    gather, table, back, turned = call(
        prepare_kernel,
        [
            struct((2 * SUB, arrivals), bf16),
            struct((arrivals + 2 * SUB, 2 * LAN), bf16),
            struct((2 * LAN, arrivals), bf16),
            struct((width, width), bf16),
        ],
        5, [padded], moved=12 * MIB,
    )(ids, pair_slots[0].T, labels, asked, weight)

    out, rows, dscore = call(
        owner_kernel,
        [struct((arrivals, half), bf16), struct((SUB, width), bf16), struct((SUB, LAN), bf16)],
        1,
        [pltpu.VMEM((2 * SUB, arrivals), bf16)]
        + [pltpu.VMEM((LAN, width), bf16)] * 2
        + [pltpu.VMEM((2 * LAN, half), bf16)]
        + [pltpu.VMEM((width, width), bf16)] * 2
        + [pltpu.VMEM((arrivals, 2 * LAN), bf16)]
        + [pltpu.VMEM((2 * SUB, 2 * LAN), bf16), pltpu.VMEM((arrivals, half), bf16)]
        + [dma((6,)), dma((4,))],
        flops=4 * 10**9, moved=14 * MIB, hbm=4, hbm_outs=1, grant=49.5,
    )(arrived, gather, weight, turned, table)
    returned = lax.all_to_all(
        out.reshape(n_rec, 2 * CAP, half), REC, split_axis=0, concat_axis=0, tiled=True
    ).reshape(arrivals, half)

    core = lax.axis_index("c").astype(i32).reshape(1)
    rows_core = width // NC

    send = call(
        send_kernel, struct((rows_core, width), bf16), 2,
        [pltpu.VMEM((LAN, width), bf16), pltpu.VMEM((rows_core, width), bf16), dma((4,))],
        flops=10**9, moved=4 * MIB, smem=1, hbm_outs=1, grant=24,
    )(1 - core, rows, dscore)
    keep = call(
        keep_kernel, struct((rows_core, width), f32), 2, [pltpu.VMEM((LAN, width), bf16)],
        flops=10**9, moved=4 * MIB, smem=1, grant=24,
    )(core, rows, dscore)
    got = lax.ppermute(send, "c", [(0, 1), (1, 0)])
    y = lax.axis_index("y").astype(i32).reshape(1)
    cols = width // NY
    summed, *sends = call(
        split_kernel,
        [struct((rows_core, cols), f32)] + [struct((rows_core, cols), bf16)] * (NY - 1), 2,
        flops=10**6, moved=4 * MIB, smem=1, grant=24,
    )(y, keep, got)
    for k in (2, 1, 3):
        summed = summed + lax.ppermute(sends[k - 1], "y", [(i, (i + k) % NY) for i in range(NY)]).astype(f32)
    summed = shifted_blocks(summed.reshape(NX, NZ * 16, cols), "x", NX)
    half_z = NZ // 2
    z = lax.axis_index("z")
    summed = summed.reshape(2, half_z, 16, cols)
    far = lax.dynamic_index_in_dim(summed, 1 - z // half_z, 0, keepdims=False).astype(bf16)
    near = lax.dynamic_index_in_dim(summed, z // half_z, 0, keepdims=False)
    far = lax.ppermute(far, "z", [(i, (i + half_z) % NZ) for i in range(NZ)])
    emb_grad = call(
        return_kernel, struct((rec_rows, width), f32), 1,
        [pltpu.VMEM((2 * rec_rows, arrivals), bf16), pltpu.VMEM((rec_rows, width), f32), dma((2,)), dma((2,))],
        flops=4 * arrivals * rec_rows * half, moved=6 * MIB, hbm=1, hbm_outs=1, grant=52,
    )(returned, back)
    emb_grad, far = lax.optimization_barrier((emb_grad, far))
    summed = near + far.astype(f32)
    blocks = []
    for k in range(1, half_z):
        block = lax.dynamic_index_in_dim(summed, (z + k) % half_z, 0, keepdims=False).astype(bf16)
        to = [(i, i // half_z * half_z + (i + k) % half_z) for i in range(NZ)]
        blocks.append(lax.ppermute(block, "z", to))
    summed = lax.dynamic_index_in_dim(summed, z % half_z, 0, keepdims=False)
    for block in blocks:
        summed = summed + block.astype(f32)
    pieces = [summed]
    for k in range(1, NY):
        pieces.append(lax.ppermute(summed, "y", [(i, (i + k) % NY) for i in range(NY)]))
    weight_part = call(join_kernel, struct((16, width), f32), NY, smem=1, flops=10**4, moved=10**5, grant=16)(y, *pieces)
    return (emb_grad[None], weight_part)


def solution(mesh):
    fine = Mesh(mesh.devices.reshape(NX, NZ, NC, NY), ("x", "z", "c", "y"))
    return jax.shard_map(
        on_device,
        mesh=fine,
        in_specs=(
            P("y", REC, None),
            P(),
            P("y", REC, None),
            P("y", REC, None),
            P("y", REC),
        ),
        out_specs=(P("y", REC, None), P(REC, None)),
        check_vma=False,
    )
```

```python
import jax
import jax.numpy as jnp
from jax import lax
from jax.experimental import pallas as pl
from jax.experimental.pallas import tpu as pltpu
from jax.sharding import Mesh, PartitionSpec as P

f32, bf16, i32 = jnp.float32, jnp.bfloat16, jnp.int32

CAP = 12
LIVE = 264
SUB = 272
LAN = 384
MARGIN = 0.5
NX, NZ, NC, NY = 4, 8, 2, 4
REC = ("x", "z", "c")
MIB = 2**20


def iota(shape, dim):
    return lax.broadcasted_iota(i32, shape, dim)


def ones_where(mask):
    return jnp.where(mask, 1.0, 0.0).astype(f32)


def nt(a, b):
    return lax.dot_general(a, b, (((1,), (1,)), ((), ())), preferred_element_type=f32)


def tn(a, b):
    return lax.dot_general(a, b, (((0,), (0,)), ((), ())), preferred_element_type=f32)


def mm(a, b):
    return jnp.dot(a, b, preferred_element_type=f32)


def bucket_tables(members_ref, padded, n_rec, rec_rows):
    blocks, most = members_ref.shape
    padded[...] = jnp.full(padded.shape, -1, i32)
    padded[:, :most] = members_ref[...]
    earlier = ones_where(iota((128, 128), 0) < iota((128, 128), 1)).astype(bf16)
    running = jnp.zeros((n_rec, 1), f32)
    out = []
    for b in range(blocks):
        ids = padded[b : b + 1, :]
        source = (lax.shift_right_arithmetic(ids, 7) * 171) >> 9
        row = ids - source * rec_rows
        source = jnp.where(ids >= 0, source, -1)
        hit = ones_where(iota((n_rec, 128), 0) == source)
        place = mm(hit.astype(bf16), earlier) + running
        running = running + jnp.sum(hit, axis=1, keepdims=True)
        out.append((source, row, hit, place))
    return out


def request_kernel(members_ref, out_ref, padded):
    n_rec = out_ref.shape[0]
    tables = bucket_tables(members_ref, padded, n_rec, LAN)
    lane = iota((n_rec, 128), 1)
    asked = jnp.zeros((n_rec, 128), f32)
    for k in range(CAP):
        found = jnp.zeros((n_rec, 128), f32)
        for source, row, hit, place in tables:
            found = found + jnp.where(place == k, hit, 0.0) * (row + 1).astype(f32)
        asked = jnp.where(lane == k, jnp.sum(found, axis=1, keepdims=True), asked)
    out_ref[...] = asked.astype(i32).reshape(out_ref.shape)


def wanted_rows(asked_ref):
    n_rec = asked_ref.shape[0]
    asked = asked_ref[...].reshape(n_rec, 1, 128).astype(f32)
    step = iota((n_rec, 2 * CAP, 128), 1)
    step = jnp.where(step >= CAP, step - CAP, step)
    mine = jnp.where(iota((n_rec, 2 * CAP, 128), 2) == step, asked, 0.0)
    wanted = jnp.sum(mine, axis=2, keepdims=True).astype(i32) - 1
    later = iota((n_rec, 2 * CAP, 1), 1) >= CAP
    return wanted + jnp.where(later & (wanted >= 0), LAN, 0)


def stack_kernel(emb_ref, out_ref):
    rows, width = emb_ref.shape
    out_ref[:rows, :] = emb_ref[:, : width // 2].astype(bf16)
    out_ref[rows:, :] = emb_ref[:, width // 2 :].astype(bf16)


def fetch_kernel(asked_ref, stacked_ref, out_hbm, out_s, sems):
    n_rec = asked_ref.shape[0]
    parts = sems.shape[0]
    rows = n_rec * 2 * CAP // parts
    wanted = wanted_rows(asked_ref)
    stores = []
    for t in range(parts):
        mine = wanted[t * n_rec // parts : (t + 1) * n_rec // parts]
        pick = ones_where(iota((n_rec // parts, 2 * CAP, 2 * LAN), 2) == mine).reshape(rows, 2 * LAN).astype(bf16)
        here = pl.ds(t * rows, rows)
        out_s[here, :] = mm(pick, stacked_ref[...]).astype(bf16)
        stores.append(pltpu.make_async_copy(out_s.at[here], out_hbm.at[here], sems.at[t]))
        stores[t].start()
    for store in stores:
        store.wait()


def prepare_kernel(
    members_ref, pairs_ref, labels_ref, asked_ref,
    gather_ref, table_ref, back_ref, padded,
):
    arrivals = gather_ref.shape[1]
    n_rec = arrivals // (2 * CAP)
    blocks, most = members_ref.shape
    tables = bucket_tables(members_ref, padded, n_rec, LAN)
    sub = iota((LAN, 128), 0)
    lane = iota((1, 128), 1)
    offset = jnp.zeros((1, 1), i32)
    offsets, lengths = [], []
    bucket = jnp.zeros((LAN, 1), f32)
    for b, (source, row, hit, place) in enumerate(tables):
        live = source >= 0
        length = jnp.sum(ones_where(live), axis=1, keepdims=True).astype(i32)
        offsets.append(offset)
        lengths.append(length)
        slot = jnp.where(live, offset + lane, -1)
        offset = offset + length
        at = jnp.sum(hit * place, axis=0, keepdims=True) + (source * (2 * CAP) + 1).astype(f32)
        bucket = bucket + jnp.sum(jnp.where(sub == slot, at, 0.0), axis=1, keepdims=True)
    bucket_col = bucket.astype(i32) - 1
    bucket_col = jnp.where(bucket_col < 0, -4096, bucket_col)
    bucket_row = jnp.transpose(jnp.broadcast_to(bucket, (LAN, 128)))[0:1, :].astype(i32) - 1
    bucket_row = jnp.where(bucket_row < 0, -4096, bucket_row)
    lanes = iota((SUB, arrivals), 1)
    gather_ref[:SUB, :] = ones_where(lanes == bucket_col[:SUB]).astype(bf16)
    gather_ref[SUB:, :] = ones_where(lanes == bucket_col[:SUB] + CAP).astype(bf16)
    rows = iota((arrivals, LAN), 0)
    table_ref[:arrivals, :LAN] = ones_where(rows == bucket_row).astype(bf16)
    table_ref[:arrivals, LAN:] = ones_where(rows == bucket_row + CAP).astype(bf16)

    col, row = iota((SUB, 1), 0), iota((1, LAN), 1)
    block_col, block_row = jnp.zeros((SUB, 1), i32), jnp.zeros((1, LAN), i32)
    count = jnp.zeros((1, LAN), f32) + lengths[0].astype(f32)
    for b in range(1, blocks):
        block_col = jnp.where(col >= offsets[b], b, block_col)
        block_row = jnp.where(row >= offsets[b], b, block_row)
        count = jnp.where(row >= offsets[b], lengths[b].astype(f32), count)
    block_col = jnp.where(col < LIVE, block_col, -1)
    block_row = jnp.where(row < LIVE, block_row, -2)
    counts = jnp.where((block_col == block_row) & (col != row), count, 0.0)
    table_ref[arrivals : arrivals + SUB, :LAN] = counts.astype(bf16)

    def packed(slots):
        at = jnp.zeros((1, 128), i32) + offsets[0]
        first = jnp.zeros((1, 128), i32)
        for b in range(1, blocks):
            at = jnp.where(slots >= b * most, offsets[b], at)
            first = jnp.where(slots >= b * most, b * most, first)
        return at + slots - first

    label = labels_ref[...].astype(f32)
    one = jnp.where(iota((SUB, 128), 0) == packed(pairs_ref[0:1, :]), 1.0, 0.0)
    two = ones_where(iota((LAN, 128), 0) == packed(pairs_ref[1:2, :])).astype(bf16)
    table_ref[arrivals : arrivals + SUB, LAN:] = nt((one * (1.0 - label)).astype(bf16), two).astype(bf16)
    table_ref[arrivals + SUB :, :LAN] = nt((one * label).astype(bf16), two).astype(bf16)
    table_ref[arrivals + SUB :, LAN:] = jnp.zeros((SUB, LAN), bf16)
    wanted = wanted_rows(asked_ref).reshape(arrivals, 1).astype(f32)
    wanted = jnp.transpose(jnp.broadcast_to(wanted, (arrivals, 128)))[0:1, :].astype(i32)
    back_ref[...] = ones_where(iota((2 * LAN, arrivals), 0) == wanted).astype(bf16)


def owner_kernel(
    arrived_ref, gather_hbm, weight_hbm, table_hbm,
    out_hbm, rows_ref, dscore_ref,
    gather_s, rows_s, right_s, stacked_s, weight_s, spread_s, terms_s, out_s, sems, out_sems,
):
    arrivals, half = arrived_ref.shape
    width = 2 * half
    terms_hbm, spread_hbm = table_hbm.at[arrivals:], table_hbm.at[:arrivals]
    loads = []
    for n, (source, target) in enumerate([
        (gather_hbm.at[:SUB], gather_s.at[:SUB]),
        (gather_hbm.at[SUB:], gather_s.at[SUB:]),
        (weight_hbm, weight_s),
        (terms_hbm, terms_s),
        (spread_hbm, spread_s),
    ]):
        loads.append(pltpu.make_async_copy(source, target, sems.at[n]))
        if n < 4:
            loads[n].start()
    loads[0].wait()
    rows_s[:SUB, :half] = mm(gather_s[:SUB, :], arrived_ref[...]).astype(bf16)
    loads[1].wait()
    rows_s[:SUB, half:] = mm(gather_s[SUB:, :], arrived_ref[...]).astype(bf16)
    rows_s[SUB:, :] = jnp.zeros((LAN - SUB, width), bf16)
    rows = rows_s[:SUB, :]
    rows_ref[...] = rows
    loads[2].wait()
    loads[4].start()
    left = mm(rows, weight_s[...]).astype(bf16)
    right_s[:SUB, :] = nt(rows, weight_s[...]).astype(bf16)
    right_s[SUB:, :] = jnp.zeros((LAN - SUB, width), bf16)
    shifted = nt(left, rows_s[...]) - MARGIN
    small = jnp.exp(-jnp.abs(shifted))
    larger = 1.0 / (1.0 + small)
    smaller = small * larger
    up = jnp.where(shifted >= 0, larger, smaller)
    down = jnp.where(shifted >= 0, smaller, larger)
    loads[3].wait()
    count = terms_s[:SUB, :LAN].astype(f32)
    plus = terms_s[:SUB, LAN:].astype(f32)
    minus = terms_s[SUB:, :LAN].astype(f32)
    dscore = jnp.where(count > 0, up / jnp.maximum(count, 1.0), 0.0) + (up * plus - down * minus)
    dscore = dscore.astype(bf16)
    dscore_ref[...] = dscore
    grad = mm(dscore, right_s[...]) + tn(dscore, left)[:SUB]
    grad = grad.astype(bf16)
    stacked_s[:SUB, :] = grad[:, :half]
    stacked_s[SUB:LAN, :] = jnp.zeros((LAN - SUB, half), bf16)
    stacked_s[LAN : LAN + SUB, :] = grad[:, half:]
    stacked_s[LAN + SUB :, :] = jnp.zeros((LAN - SUB, half), bf16)
    loads[4].wait()
    parts = out_sems.shape[0]
    size = arrivals // parts
    stores = []
    for t in range(parts):
        here = pl.ds(t * size, size)
        out_s[here, :] = mm(spread_s[here, :], stacked_s[...]).astype(bf16)
        stores.append(pltpu.make_async_copy(out_s.at[here], out_hbm.at[here], out_sems.at[t]))
        stores[t].start()
    for store in stores:
        store.wait()


def half_term(core, rows_ref, dscore_ref, rows_s):
    width = rows_ref.shape[1]
    rows_s[:SUB, :] = rows_ref[...]
    rows_s[SUB:, :] = jnp.zeros((LAN - SUB, width), bf16)
    carried = mm(dscore_ref[...], rows_s[...]).astype(bf16)
    tile = 256
    for t in range(width // tile):
        part = tn(rows_s[:SUB, t * tile : (t + 1) * tile], carried)
        part = part.reshape(tile // 32, 2, 16, width)
        even = jnp.broadcast_to(core, (tile // 32, 16, width)) == 0
        yield pl.ds(t * tile // 2, tile // 2), jnp.where(even, part[:, 0], part[:, 1]).reshape(tile // 2, width)


def keep_kernel(core_ref, rows_ref, dscore_ref, out_ref, rows_s):
    for place, part in half_term(core_ref[0], rows_ref, dscore_ref, rows_s):
        out_ref[place, :] = part


def send_kernel(core_ref, rows_ref, dscore_ref, out_hbm, rows_s, out_s, sems):
    stores = []
    for n, (place, part) in enumerate(half_term(core_ref[0], rows_ref, dscore_ref, rows_s)):
        out_s[place, :] = part.astype(bf16)
        stores.append(pltpu.make_async_copy(out_s.at[place], out_hbm.at[place], sems.at[n]))
        stores[n].start()
    for store in stores:
        store.wait()


def split_kernel(y_ref, keep_ref, got_ref, own_ref, *send_refs):
    size = own_ref.shape[1]
    for k in range(NY):
        at = pl.multiple_of(((y_ref[0] + k) % NY) * size, size)
        part = keep_ref[:, pl.ds(at, size)] + got_ref[:, pl.ds(at, size)].astype(f32)
        if k == 0:
            own_ref[...] = part
        else:
            send_refs[k - 1][...] = part.astype(bf16)


def join_kernel(y_ref, *refs):
    *piece_refs, out_ref = refs
    size = piece_refs[0].shape[1]
    for k, piece_ref in enumerate(piece_refs):
        at = pl.multiple_of(((y_ref[0] + NY - k) % NY) * size, size)
        out_ref[:, pl.ds(at, size)] = piece_ref[...]


def return_kernel(back_ref, pick_hbm, out_hbm, pick_s, out_s, in_sems, out_sems):
    half = back_ref.shape[1]
    rows = out_s.shape[0]
    loads = [
        pltpu.make_async_copy(pick_hbm.at[pl.ds(h * rows, rows)], pick_s.at[pl.ds(h * rows, rows)], in_sems.at[h])
        for h in range(2)
    ]
    stores = [
        pltpu.make_async_copy(
            out_s.at[:, pl.ds(h * half, half)], out_hbm.at[:, pl.ds(h * half, half)], out_sems.at[h]
        )
        for h in range(2)
    ]
    for load in loads:
        load.start()
    for h in range(2):
        loads[h].wait()
        out_s[:, h * half : (h + 1) * half] = mm(pick_s[h * rows : (h + 1) * rows, :], back_ref[...])
        stores[h].start()
    for store in stores:
        store.wait()


def vmem(n):
    return [pl.BlockSpec(memory_space=pltpu.VMEM)] * n


def call(kernel, outs, n_in, scratch=(), flops=0, moved=0, smem=0, hbm=0, hbm_outs=0, grant=60):
    single = not isinstance(outs, (list, tuple))
    n_out = 1 if single else len(outs)
    out_specs = [pl.BlockSpec(memory_space=pltpu.HBM)] * hbm_outs + vmem(n_out - hbm_outs)
    return pl.pallas_call(
        kernel,
        out_shape=outs,
        in_specs=[pl.BlockSpec(memory_space=pltpu.SMEM)] * smem + vmem(n_in) + [pl.BlockSpec(memory_space=pltpu.HBM)] * hbm,
        out_specs=out_specs[0] if single else out_specs,
        scratch_shapes=list(scratch),
        compiler_params=pltpu.CompilerParams(vmem_limit_bytes=int(grant * MIB)),
        cost_estimate=pl.CostEstimate(flops=flops, bytes_accessed=moved, transcendentals=0),
    )


def shifted_blocks(value, axis, size):
    here = lax.axis_index(axis)
    got = []
    for k in (2, 1, 3):
        block = lax.dynamic_index_in_dim(value, (here + k) % size, 0, keepdims=False).astype(bf16)
        got.append(lax.ppermute(block, axis, [(i, (i + k) % size) for i in range(size)]))
    total = lax.dynamic_index_in_dim(value, here, 0, keepdims=False)
    for block in got:
        total = total + block.astype(f32)
    return total


def on_device(embeddings, weight, members, pair_slots, labels):
    n_rec = NX * NZ * NC
    rec_rows, width = embeddings.shape[1:]
    half = width // 2
    arrivals = n_rec * 2 * CAP
    struct = jax.ShapeDtypeStruct
    ids = members[0]
    padded = pltpu.VMEM((ids.shape[0], 128), i32)

    requests = call(request_kernel, struct((n_rec, 1, 128), i32), 1, [padded], grant=16)(ids)
    asked = lax.all_to_all(requests, REC, split_axis=0, concat_axis=0, tiled=True)
    dma = pltpu.SemaphoreType.DMA
    stacked = call(
        stack_kernel, struct((2 * rec_rows, half), bf16), 1, flops=10**6, moved=3 * MIB, grant=16
    )(embeddings[0])
    found = call(
        fetch_kernel, struct((arrivals, half), bf16), 2,
        [pltpu.VMEM((arrivals, half), bf16), dma((4,))],
        flops=4 * arrivals * rec_rows * half, moved=3 * MIB, hbm_outs=1, grant=32,
    )(asked, stacked)
    arrived = lax.all_to_all(
        found.reshape(n_rec, 2 * CAP, half), REC, split_axis=0, concat_axis=0, tiled=True
    ).reshape(arrivals, half)
    gather, table, back = call(
        prepare_kernel,
        [
            struct((2 * SUB, arrivals), bf16),
            struct((arrivals + 2 * SUB, 2 * LAN), bf16),
            struct((2 * LAN, arrivals), bf16),
        ],
        4, [padded], moved=8 * MIB,
    )(ids, pair_slots[0].T, labels, asked)

    out, rows, dscore = call(
        owner_kernel,
        [struct((arrivals, half), bf16), struct((SUB, width), bf16), struct((SUB, LAN), bf16)],
        1,
        [pltpu.VMEM((2 * SUB, arrivals), bf16)]
        + [pltpu.VMEM((LAN, width), bf16)] * 2
        + [pltpu.VMEM((2 * LAN, half), bf16), pltpu.VMEM((width, width), bf16), pltpu.VMEM((arrivals, 2 * LAN), bf16)]
        + [pltpu.VMEM((2 * SUB, 2 * LAN), bf16), pltpu.VMEM((arrivals, half), bf16)]
        + [dma((5,)), dma((4,))],
        flops=4 * 10**9, moved=12 * MIB, hbm=3, hbm_outs=1, grant=49.5,
    )(arrived, gather, weight, table)
    returned = lax.all_to_all(
        out.reshape(n_rec, 2 * CAP, half), REC, split_axis=0, concat_axis=0, tiled=True
    ).reshape(arrivals, half)

    core = lax.axis_index("c").astype(i32).reshape(1)
    rows_core = width // NC

    send = call(
        send_kernel, struct((rows_core, width), bf16), 2,
        [pltpu.VMEM((LAN, width), bf16), pltpu.VMEM((rows_core, width), bf16), dma((4,))],
        flops=10**9, moved=4 * MIB, smem=1, hbm_outs=1, grant=24,
    )(1 - core, rows, dscore)
    keep = call(
        keep_kernel, struct((rows_core, width), f32), 2, [pltpu.VMEM((LAN, width), bf16)],
        flops=10**9, moved=4 * MIB, smem=1, grant=24,
    )(core, rows, dscore)
    got = lax.ppermute(send, "c", [(0, 1), (1, 0)])
    y = lax.axis_index("y").astype(i32).reshape(1)
    cols = width // NY
    summed, *sends = call(
        split_kernel,
        [struct((rows_core, cols), f32)] + [struct((rows_core, cols), bf16)] * (NY - 1), 2,
        flops=10**6, moved=4 * MIB, smem=1, grant=24,
    )(y, keep, got)
    for k in (2, 1, 3):
        summed = summed + lax.ppermute(sends[k - 1], "y", [(i, (i + k) % NY) for i in range(NY)]).astype(f32)
    summed = shifted_blocks(summed.reshape(NX, NZ * 16, cols), "x", NX)
    half_z = NZ // 2
    z = lax.axis_index("z")
    summed = summed.reshape(2, half_z, 16, cols)
    far = lax.dynamic_index_in_dim(summed, 1 - z // half_z, 0, keepdims=False).astype(bf16)
    near = lax.dynamic_index_in_dim(summed, z // half_z, 0, keepdims=False)
    far = lax.ppermute(far, "z", [(i, (i + half_z) % NZ) for i in range(NZ)])
    emb_grad = call(
        return_kernel, struct((rec_rows, width), f32), 1,
        [pltpu.VMEM((2 * rec_rows, arrivals), bf16), pltpu.VMEM((rec_rows, width), f32), dma((2,)), dma((2,))],
        flops=4 * arrivals * rec_rows * half, moved=6 * MIB, hbm=1, hbm_outs=1, grant=52,
    )(returned, back)
    emb_grad, far = lax.optimization_barrier((emb_grad, far))
    summed = near + far.astype(f32)
    blocks = []
    for k in range(1, half_z):
        block = lax.dynamic_index_in_dim(summed, (z + k) % half_z, 0, keepdims=False).astype(bf16)
        to = [(i, i // half_z * half_z + (i + k) % half_z) for i in range(NZ)]
        blocks.append(lax.ppermute(block, "z", to))
    summed = lax.dynamic_index_in_dim(summed, z % half_z, 0, keepdims=False)
    for block in blocks:
        summed = summed + block.astype(f32)
    pieces = [summed]
    for k in range(1, NY):
        pieces.append(lax.ppermute(summed, "y", [(i, (i + k) % NY) for i in range(NY)]))
    weight_part = call(join_kernel, struct((16, width), f32), NY, smem=1, flops=10**4, moved=10**5, grant=16)(y, *pieces)
    return (emb_grad[None], weight_part)


def solution(mesh):
    fine = Mesh(mesh.devices.reshape(NX, NZ, NC, NY), ("x", "z", "c", "y"))
    return jax.shard_map(
        on_device,
        mesh=fine,
        in_specs=(
            P("y", REC, None),
            P(),
            P("y", REC, None),
            P("y", REC, None),
            P("y", REC),
        ),
        out_specs=(P("y", REC, None), P(REC, None)),
        check_vma=False,
    )
```
